32 devices in a mesh: row: 16 (over z, y, x), col: 2 (over core).
Axes of the slice: x: 2, y: 2, z: 4, core: 2. Of those that a mesh axis runs over, the one named last changes fastest.
Arguments:
- embeddings: bfloat16 [16384, 2048], P(('row', 'col')), may hold values from -6 to 6
- inverse_scales: float32 [2048], replicated, may hold values from 0.0039774757 to 0.059662133
- matches: int32 [16384, 2], replicated, may hold values from 0 to 16383
Outputs:
- trailing: float32 [16384, 4096], P('row', 'col')
- factor: float32 [16384, 1024], P(('row', 'col'))
The draws below stay inside these ranges and needn't reach their ends.
Inputs may be any that keep to these rules, and one draw needn't show every extreme that they name: `matches`: candidate indices of the winner and the loser of each match.
All inputs are finite; a program needn't handle non-finite values.
Results may differ from the reference program's by a relative error of at most 0.0065.
Values may be sent and summed in bfloat16 or wider, within the bound.
No kernel may reach another device: no remote copies, remote signals or barrier semaphores. Data moves between devices by JAX's collectives and lax.ppermute only.
A program may use at most 128 MiB of HBM per device.

```python
import math
import jax
import jax.numpy as jnp
from jax import lax

R_DEV = 1024
EMBED = 2048
PANEL = 1024
STOPS = 4
CANDIDATES = 16384
MATCHES = 16384
SLICE = 512
PANEL_SHARE = 64
N_ROW = 16
N_COL = 2


def plant(array, stream_key, least, largest):
    place = [jax.random.randint(jax.random.fold_in(stream_key, axis), (), 0, length) for axis, length in enumerate(array.shape)]
    longest = array.shape.index(max(array.shape))
    neighbour = place[:longest] + [(place[longest] + 1) % array.shape[longest]] + place[longest + 1:]
    return array.at[tuple(place)].set(least).at[tuple(neighbour)].set(largest)


def levels(own_key, dims, cuts, low, top_value):
    level = 1.0
    for dim, shards_of in cuts:
        heights = jax.random.uniform(jax.random.fold_in(jax.random.fold_in(own_key, 6), dim), (shards_of,), jnp.float32, low / len(cuts), top_value / len(cuts))
        level = level * jnp.repeat(jnp.exp(heights), dims[dim] // shards_of).reshape((-1,) + (1,) * (len(dims) - 1 - dim))
    return level


def bell_draw(own_key, shape, scale, bound, split=(), held_as=jnp.bfloat16):
    entries = jax.random.normal(own_key, shape, jnp.float32) * scale
    if len(split) > 0:
        entries = levels(own_key, shape, split, -0.22, 0.18) * entries
    return jnp.clip(entries, min=-bound, max=bound).astype(held_as)


def setup_inputs(seed: int = 0) -> dict:
    keys = jax.random.split(jax.random.key(seed), 4)
    return {
        "embeddings": bell_draw(keys[0], (CANDIDATES, EMBED), 1.0, 6.0, ((0, 32),)),
        "inverse_scales": jnp.clip(jnp.exp(jax.random.uniform(keys[1], (EMBED,), jnp.float32, math.log(0.0039774757), math.log(0.059662133))), 0.0039774757, 0.059662133),
        "matches": plant(jax.random.randint(keys[2], (MATCHES, 2), 0, CANDIDATES), jax.random.fold_in(keys[2], 1), 0, CANDIDATES - 1).astype(jnp.int32),
    }


def squares_of(scaled):
    values = scaled.astype(jnp.float32)
    return jnp.sum(values * values, axis=1)

def kernel_block(left, left_sq, right, right_sq):
    inner = jnp.dot(left.astype(jnp.float32), right.T.astype(jnp.float32), preferred_element_type=jnp.float32)
    return jnp.exp(-0.5 * (left_sq[:, None] + right_sq[None, :] - 2.0 * inner))

def match_counts(identity, matches):
    total = matches.shape[0]
    group_rows = math.gcd(total, 1024)
    grouped = matches.reshape(total // group_rows, group_rows, 2)

    def accumulate(carry, group):
        hits = (group[:, 0:1] == identity[None, :]).astype(jnp.float32)
        hits = hits + (group[:, 1:2] == identity[None, :]).astype(jnp.float32)
        return (carry + jnp.sum(hits, axis=0), None)
    counts, unused = lax.scan(accumulate, jnp.zeros(identity.shape, jnp.float32), grouped)
    return 0.1 + 0.5 * counts

def reference(embeddings, inverse_scales, matches):
    scaled = (embeddings.astype(jnp.float32) * inverse_scales[None, :]).astype(jnp.bfloat16)
    squares = squares_of(scaled)
    extras = match_counts(jnp.arange(CANDIDATES, dtype=jnp.int32), matches)
    panel_ids = (jnp.arange(N_ROW, dtype=jnp.int32)[:, None] * R_DEV + jnp.arange(PANEL_SHARE, dtype=jnp.int32)[None, :]).reshape(-1)
    panel_scaled = scaled[panel_ids]
    panel_sq = squares[panel_ids]
    diagonal = kernel_block(panel_scaled, panel_sq, panel_scaled, panel_sq) + jnp.diag(extras[panel_ids])
    lower = jnp.linalg.cholesky(diagonal)
    block_scaled = scaled.reshape(N_ROW, R_DEV, EMBED)
    block_sq = squares.reshape(N_ROW, R_DEV)
    block_extra = extras.reshape(N_ROW, R_DEV)

    def factor_rows(index):
        rows = kernel_block(block_scaled[index], block_sq[index], panel_scaled, panel_sq)
        identity = index * R_DEV + jnp.arange(R_DEV, dtype=jnp.int32)
        rows = rows + jnp.where(identity[:, None] == panel_ids[None, :], block_extra[index][:, None], 0.0)
        return lax.linalg.triangular_solve(lower, rows, left_side=False, lower=True, transpose_a=True)
    factor_all = lax.map(factor_rows, jnp.arange(N_ROW, dtype=jnp.int32))

    def trailing_rows(index):
        pieces = []
        for stop in range(STOPS):
            visit = (index - stop) % N_ROW
            tile = kernel_block(block_scaled[index], block_sq[index], block_scaled[visit], block_sq[visit])
            tile = tile - jnp.dot(factor_all[index], factor_all[visit].T, precision=lax.Precision.HIGHEST)
            if stop == 0:
                tile = tile + jnp.diag(block_extra[index])
            pieces.append(tile.reshape(R_DEV, N_COL, SLICE))
        return jnp.stack(pieces, axis=2).reshape(R_DEV, N_COL * STOPS * SLICE)
    trailing = lax.map(trailing_rows, jnp.arange(N_ROW, dtype=jnp.int32)).reshape(CANDIDATES, STOPS * R_DEV)
    return (trailing, factor_all.reshape(CANDIDATES, PANEL))
```

```python
import functools

import jax
import jax.numpy as jnp
from jax import lax
from jax.experimental import pallas as pl
from jax.experimental.pallas import tpu as pltpu
from jax.sharding import PartitionSpec as P

PANEL = 1024
STOPS = 4
LAYER = 4
BLOCK = 128
GROUP = 8
BAND = 32
CHUNK = 256
VMEM_BYTES = 56 * 1024 * 1024

F32 = jnp.float32
BF16 = jnp.bfloat16
NT = (((1,), (1,)), ((), ()))
NN = (((1,), (0,)), ((), ()))


def rotated(block, axis, distance):
    count = lax.axis_size(axis)
    return lax.ppermute(block, axis, [(i, (i + distance) % count) for i in range(count)])


def split(values):
    high = values.astype(BF16)
    low = (values - high.astype(F32)).astype(BF16)
    return high, low


def dot(left, right, dims):
    return lax.dot_general(left, right, dims, preferred_element_type=F32)


def dot3(left, right, dims):
    (lh, ll), (rh, rl) = left, right
    return dot(lh, rh, dims) + (dot(lh, rl, dims) + dot(ll, rh, dims))


def half_squares(block):
    values = block.astype(F32)
    return 0.5 * jnp.sum(values * values, axis=1, keepdims=True)


def reciprocal(values):
    return pl.reciprocal(values, approx=True)


def fetched(source, target, sem):
    copy = pltpu.make_async_copy(source, target, sem)
    copy.start()
    return copy


def as_row(column):
    return jnp.transpose(jnp.broadcast_to(column, (column.shape[0], 128)))[0:1, :]


def iota(shape, dim):
    return lax.broadcasted_iota(jnp.int32, shape, dim)


def extras_kernel(chunk, matches_ref, out_ref):
    high_count = out_ref.shape[0]

    def step(i, total):
        for side in range(2):
            ids = matches_ref[side : side + 1, pl.ds(pl.multiple_of(i * chunk, chunk), chunk)]
            high = lax.shift_right_logical(ids, 7)
            low = jnp.bitwise_and(ids, 127)
            high_hot = jnp.where(iota((high_count, chunk), 0) == high, 1.0, 0.0).astype(BF16)
            low_hot = jnp.where(iota((128, chunk), 0) == low, 1.0, 0.0).astype(BF16)
            total = total + dot(high_hot, low_hot, NT)
        return total

    steps = matches_ref.shape[1] // chunk
    counts = lax.fori_loop(0, steps, step, jnp.zeros(out_ref.shape, F32))
    out_ref[...] = 0.1 + 0.5 * counts


def match_extras(matches, candidates):
    total = matches.shape[0]
    return pl.pallas_call(
        functools.partial(extras_kernel, min(total, 1024)),
        out_shape=jax.ShapeDtypeStruct((candidates // 128, 128), F32),
        in_specs=[pl.BlockSpec(memory_space=pltpu.VMEM)],
        out_specs=pl.BlockSpec(memory_space=pltpu.VMEM),
        cost_estimate=pl.CostEstimate(
            flops=8_000_000_000, bytes_accessed=total * 8, transcendentals=0
        ),
        compiler_params=pltpu.CompilerParams(vmem_limit_bytes=VMEM_BYTES),
        name="match_extras",
    )(matches.T)


def factor_block(diagonal, store):
    count = BLOCK // GROUP
    shape = (GROUP, BLOCK)
    sub = iota(shape, 0)
    lane = iota(shape, 1)
    rows = [diagonal[GROUP * i : GROUP * (i + 1), :] for i in range(count)]

    def column(values, index):
        return jnp.broadcast_to(values[:, index : index + 1], shape)

    def line(values, index):
        return jnp.broadcast_to(values[index : index + 1, :], shape)

    def pick(flags, values):
        result = values[0]
        for flag, value in zip(flags[1:], values[1:]):
            result = jnp.where(flag, value, result)
        return result

    at = [sub == j for j in range(GROUP)]
    for m in range(count):
        start = GROUP * m
        inside = (lane >= start) & (lane < start + GROUP)
        cols = [column(rows[m], start + b) for b in range(GROUP)]
        cell = {(a, b): line(cols[b], a) for b in range(GROUP) for a in range(b + 1)}
        held = jnp.where(inside, jnp.where(lane == start + sub, 1.0, 0.0), rows[m])
        lines = [line(held, j) for j in range(GROUP)]
        band_end = (m * GROUP // BAND + 1) * BAND
        last = (m + 1) * GROUP == band_end
        if start % BAND == 0:
            band = []
        if not last:
            near = [column(rows[m + 1], start + b) for b in range(GROUP)]
            change = None
        scaled_lines, factors, solved_lines, pivots = [], {}, [], []
        for j in range(0, GROUP, 2):
            top, cross, low = cell[j, j], cell[j, j + 1], cell[j + 1, j + 1]
            det = top * low - cross * cross
            inverse = reciprocal(det)
            tops, crosses, lows = top * inverse, cross * inverse, low * inverse
            for b in range(j + 2, GROUP):
                u, v = cell[j, b], cell[j + 1, b]
                factors[j, b] = u * lows - v * crosses
                factors[j + 1, b] = v * tops - u * crosses
            for b in range(j + 2, GROUP):
                for a in range(j + 2, b + 1):
                    part = factors[j, a] * cell[j, b] + factors[j + 1, a] * cell[j + 1, b]
                    cell[a, b] = cell[a, b] - part
            if not last:
                weight1 = near[j] * lows - near[j + 1] * crosses
                weight2 = near[j + 1] * tops - near[j] * crosses
                part = weight1 * lines[j] + weight2 * lines[j + 1]
                change = part if change is None else change + part
                for b in range(j + 2, GROUP):
                    near[b] = near[b] - (near[j] * factors[j, b] + near[j + 1] * factors[j + 1, b])
            for b in range(j + 2, GROUP):
                part = factors[j, b] * lines[j] + factors[j + 1, b] * lines[j + 1]
                lines[b] = lines[b] - part
            solved_lines.append(lines[j] * lows - lines[j + 1] * crosses)
            solved_lines.append(lines[j + 1] * tops - lines[j] * crosses)
            top_inverse = reciprocal(top)
            scaled_lines += [lines[j], lines[j + 1] - cross * top_inverse * lines[j]]
            pivots += [top, det * top_inverse]
        done = pick(at, scaled_lines) * lax.rsqrt(pick(at, pivots))
        store(m, jnp.where(lane < start + GROUP, done, 0.0))
        band.append(jnp.where((lane >= start + GROUP) & (lane < band_end), 0.0, done))
        if not last:
            rows[m + 1] = jnp.where(inside, 0.0, rows[m + 1]) - change
            others = range(m + 2, band_end // GROUP)
            for j in range(GROUP - 4, -1, -2) if len(others) > 0 else ():
                for b in range(j + 2, GROUP):
                    solved_lines[j] = solved_lines[j] - factors[j, b] * solved_lines[b]
                    solved_lines[j + 1] = solved_lines[j + 1] - factors[j + 1, b] * solved_lines[b]
            for i in others:
                terms = [column(rows[i], start + j) * solved_lines[j] for j in range(GROUP)]
                while len(terms) > 1:
                    terms = [a + b for a, b in zip(terms[0::2], terms[1::2])]
                rows[i] = jnp.where(inside, 0.0, rows[i]) - terms[0]
        elif m + 1 < count:
            finished = split(jnp.concatenate(band, axis=0))
            held_out = (lane >= band_end - BAND) & (lane < band_end)
            rest = [jnp.where(held_out, rows[i], 0.0) for i in range(m + 1, count)]
            factor = dot3(split(jnp.concatenate(rest, axis=0)), finished, NT)
            change = dot3(split(factor), finished, NN)
            for i in range(m + 1, count):
                first = GROUP * (i - m - 1)
                rows[i] = jnp.where(held_out, 0.0, rows[i]) - change[first : first + GROUP, :]


def lower_kernel(cols, layers, share, place_ref, *refs):
    pieces = refs[: cols * LAYER]
    extra_ref, high_ref, low_ref, sq_ref, panel_ref = refs[cols * LAYER : cols * LAYER + 5]
    panel, work, ahead, inv, inv_high, inv_low, sq_col, sems, panel_sem = refs[cols * LAYER + 5 :]
    size = work.shape[0]
    row = place_ref[0]
    layer, spot = lax.div(row, LAYER), lax.rem(row, LAYER)
    copies = []
    for e in range(cols):
        for d in range(LAYER):
            for back in range(layers):
                from_spot = spot + d - 2 * jnp.bitwise_and(spot, d)
                block = lax.rem(layer - back + layers, layers) * LAYER + from_spot
                there = pl.ds(pl.multiple_of(block * share, share), share)
                copies.append(
                    fetched(
                        pieces[e * LAYER + d].at[back * share : (back + 1) * share, :],
                        panel.at[e, there, :],
                        sems.at[len(copies)],
                    )
                )
    for copy in copies:
        copy.wait()
    saved = fetched(panel, panel_ref, panel_sem)
    tile = CHUNK
    for r in range(size // tile):
        rows = slice(r * tile, (r + 1) * tile)
        total = half_squares(panel[0, rows, :])
        for e in range(1, cols):
            total = total + half_squares(panel[e, rows, :])
        sq_col[rows, :] = jnp.broadcast_to(total, (tile, 128))
    sq_ref[...] = jnp.transpose(sq_col[...])[0:8, :]
    for r in range(size // tile):
        rows = slice(r * tile, (r + 1) * tile)
        inner = dot(panel[0, rows, :], panel[0], NT)
        for e in range(1, cols):
            inner = inner + dot(panel[e, rows, :], panel[e], NT)
        block = jnp.exp(inner - sq_col[rows, 0:1] - sq_ref[0:1, :])
        on_diagonal = iota((tile, size), 0) + r * tile == iota((tile, size), 1)
        work[rows, :] = block + jnp.where(on_diagonal, extra_ref[...], 0.0)

    steps = size // BLOCK

    def place_of(k):
        return pl.ds(pl.multiple_of(k * BLOCK, BLOCK), BLOCK)

    def store(m, values):
        inv[GROUP * m : GROUP * (m + 1), :] = values

    def look_ahead(k):
        here, there = place_of(k), place_of(lax.rem(k + 1, steps))
        inverse = split(inv[...])
        inv_high[...], inv_low[...] = inverse
        factor = split(dot3(split(work[there, here]), inverse, NT))
        ahead[...] = work[there, there] - dot3(factor, factor, NT)

    def finish_line(k):
        here = place_of(k)
        inverse = (inv_high[...], inv_low[...])
        line = dot3(inverse, split(work[here, :]), NN)
        inside = lax.shift_right_logical(iota((BLOCK, size), 1), 7) == k
        whole = inv_high[...].astype(F32) + inv_low[...].astype(F32)
        line = jnp.where(inside, jnp.concatenate([whole] * steps, axis=1), line)
        work[here, :] = line
        return split(line)

    factor_block(work[0:BLOCK, 0:BLOCK], store)
    look_ahead(0)

    def eliminate(k, carry):
        here = place_of(k - 1)
        diagonal = ahead[...]
        inverse = (inv_high[...], inv_low[...])
        line = finish_line(k - 1)
        inside = lax.shift_right_logical(iota((1, size), 1), 7) == k - 1
        for d in range(steps - 1):
            there = place_of(lax.rem(k + d, steps))
            valid = k + d < steps
            factor = dot3(split(work[there, here]), inverse, NT)
            factor = split(jnp.where(valid, factor, 0.0))
            keep = jnp.where(inside & valid, 0.0, 1.0)
            work[there, :] = work[there, :] * keep - dot3(factor, line, NN)
        factor_block(diagonal, store)
        look_ahead(k)
        return carry

    lax.fori_loop(1, steps, eliminate, 0)
    finish_line(steps - 1)
    for r in range(steps):
        rows = slice(r * BLOCK, (r + 1) * BLOCK)
        kept = iota((BLOCK, size), 0) + r * BLOCK >= iota((BLOCK, size), 1)
        high_ref[rows, :], low_ref[rows, :] = split(jnp.where(kept, work[rows, :], 0.0))
    saved.wait()


def inverse_lower(place, pieces, panel_extra, share):
    size = panel_extra.shape[1]
    cols = len(pieces)
    held, width = pieces[0][0].shape
    layers = held // share
    flat = [piece for group in pieces for piece in group]
    vmem = pl.BlockSpec(memory_space=pltpu.VMEM)
    anywhere = pl.BlockSpec(memory_space=pl.ANY)
    return pl.pallas_call(
        functools.partial(lower_kernel, cols, layers, share),
        out_shape=(
            jax.ShapeDtypeStruct((size, size), BF16),
            jax.ShapeDtypeStruct((size, size), BF16),
            jax.ShapeDtypeStruct((8, size), F32),
            jax.ShapeDtypeStruct((cols, size, width), BF16),
        ),
        in_specs=[pl.BlockSpec(memory_space=pltpu.SMEM)] + [anywhere] * len(flat) + [vmem],
        out_specs=(vmem, vmem, vmem, anywhere),
        scratch_shapes=[
            pltpu.VMEM((cols, size, width), BF16),
            pltpu.VMEM((size, size), F32),
            pltpu.VMEM((BLOCK, BLOCK), F32),
            pltpu.VMEM((BLOCK, BLOCK), F32),
            pltpu.VMEM((BLOCK, BLOCK), BF16),
            pltpu.VMEM((BLOCK, BLOCK), BF16),
            pltpu.VMEM((size, 128), F32),
            pltpu.SemaphoreType.DMA((cols * LAYER * layers,)),
            pltpu.SemaphoreType.DMA,
        ],
        cost_estimate=pl.CostEstimate(
            flops=50_000_000_000, bytes_accessed=8 * size * size, transcendentals=size * size
        ),
        compiler_params=pltpu.CompilerParams(vmem_limit_bytes=VMEM_BYTES),
        name="inverse_lower",
    )(place, *flat, panel_extra)


def solved(values, high_ref, low_ref):
    high, low = split(values)
    size = high.shape[1]
    parts = []
    for j in range(size // CHUNK):
        upto = CHUNK * (j + 1)
        rows = slice(CHUNK * j, upto)
        inverse = (high_ref[rows, :upto], low_ref[rows, :upto])
        parts.append(dot3((high[:, :upto], low[:, :upto]), inverse, NT))
    return jnp.concatenate(parts, axis=1)


def panel_rows(x_ref, rows, panel, features, half, sq_row):
    inner = None
    width = panel.shape[2]
    for e, start in enumerate(features):
        lanes = pl.ds(pl.multiple_of(start * width, width), width)
        part = dot(x_ref[rows, lanes], panel[e], NT)
        inner = part if inner is None else inner + part
    return jnp.exp(inner - half - sq_row)


def panel_hits(values, first_local, row, share, extra_ref):
    local = iota(values.shape, 0) + first_local
    hit = (local + row * share == iota(values.shape, 1)) & (local < share)
    return values + jnp.where(hit, extra_ref[...], 0.0)


def own_kernel(cols, share, place_ref, *refs):
    slices = refs[:cols]
    panel_hbm, high_hbm, low_hbm, sq_ref, panel_extra_ref, own_extra_ref = refs[cols : cols + 6]
    out_hbm, factor_hbm, block_high_hbm, block_low_hbm, half_ref = refs[cols + 6 : cols + 11]
    held, panel, high, low, block_high, block_low, factor, tiles, sems = refs[cols + 11 :]
    row, col = place_ref[0], place_ref[1]
    count = held.shape[0] // cols
    chunk = min(CHUNK, count)
    places = [lax.rem(col - d + cols, cols) for d in range(cols)]
    starts = [pl.multiple_of(place * count, count) for place in places]

    copies = [fetched(slices[0], held.at[0:count, :], sems.at[0])]
    copies.append(fetched(panel_hbm, panel, sems.at[1]))
    copies += [fetched(high_hbm, high, sems.at[2]), fetched(low_hbm, low, sems.at[3])]
    for d in range(1, cols):
        copies.append(fetched(slices[d], held.at[d * count : (d + 1) * count, :], sems.at[3 + d]))
    per = count // chunk
    block_rows = cols * count
    for copy in copies[:2] + copies[4:]:
        copy.wait()
    sq_row = sq_ref[0:1, :]

    def first_row(r):
        place = lax.rem(col - lax.div(r, per) + cols, cols)
        return pl.multiple_of(place * count + lax.rem(r, per) * chunk, chunk)

    def rows_step(r, carry):
        rows = pl.ds(pl.multiple_of(r * chunk, chunk), chunk)
        first = first_row(r)
        there = pl.ds(first, chunk)
        half = half_squares(held[rows, :])
        half_ref[there, :] = jnp.broadcast_to(half, (chunk, 128))
        block = panel_rows(held, rows, panel, places, half, sq_row)
        block = panel_hits(block, first, row, share, panel_extra_ref)

        @pl.when(r == 0)
        def _():
            copies[2].wait()
            copies[3].wait()

        values = solved(block, high, low)
        factor[rows, :] = values
        block_high[there, :], block_low[there, :] = split(values)
        return carry

    lax.fori_loop(0, cols * per, rows_step, 0)
    outs = [
        fetched(factor.at[0:count, :], factor_hbm, sems.at[4 + cols]),
        fetched(block_high, block_high_hbm, sems.at[5 + cols]),
        fetched(block_low, block_low_hbm, sems.at[6 + cols]),
    ]
    mine = pl.ds(starts[0], count)
    own_row = as_row(half_ref[mine, 0:1])

    def tile_step(r, carry):
        rows = pl.ds(pl.multiple_of(r * chunk, chunk), chunk)
        there = pl.ds(first_row(r), chunk)
        inner = dot(held[rows, :], held[0:count, :], NT)
        values = jnp.exp(inner - half_ref[there, 0:1] - own_row)
        own_factor = (block_high[mine, :], block_low[mine, :])
        values = values - dot3((block_high[there, :], block_low[there, :]), own_factor, NT)
        same = iota((chunk, count), 0) + r * chunk == iota((chunk, count), 1)
        tiles[there, :] = values + jnp.where(same, own_extra_ref[...], 0.0)
        return carry

    lax.fori_loop(0, cols * per, tile_step, 0)
    outs.append(fetched(tiles, out_hbm.at[:, 0:count], sems.at[3 + cols]))
    for copy in outs:
        copy.wait()


def own_rows(place, slices, panel, high, low, sq, panel_extra, own_extra, share):
    cols = len(slices)
    (count, embed), size = slices[0].shape, high.shape[0]
    block_rows = count * cols
    vmem = pl.BlockSpec(memory_space=pltpu.VMEM)
    anywhere = pl.BlockSpec(memory_space=pl.ANY)
    return pl.pallas_call(
        functools.partial(own_kernel, cols, share),
        out_shape=(
            jax.ShapeDtypeStruct((block_rows, STOPS * count), F32),
            jax.ShapeDtypeStruct((count, size), F32),
            jax.ShapeDtypeStruct((block_rows, size), BF16),
            jax.ShapeDtypeStruct((block_rows, size), BF16),
            jax.ShapeDtypeStruct((block_rows, 128), F32),
        ),
        in_specs=[pl.BlockSpec(memory_space=pltpu.SMEM)] + [anywhere] * (cols + 3) + [vmem] * 3,
        out_specs=(anywhere, anywhere, anywhere, anywhere, vmem),
        scratch_shapes=[
            pltpu.VMEM((block_rows, embed), BF16),
            pltpu.VMEM(panel.shape, BF16),
            pltpu.VMEM((size, size), BF16),
            pltpu.VMEM((size, size), BF16),
            pltpu.VMEM((block_rows, size), BF16),
            pltpu.VMEM((block_rows, size), BF16),
            pltpu.VMEM((block_rows, size), F32),
            pltpu.VMEM((block_rows, count), F32),
            pltpu.SemaphoreType.DMA((cols + 7,)),
        ],
        cost_estimate=pl.CostEstimate(
            flops=block_rows * size, bytes_accessed=block_rows * size, transcendentals=0
        ),
        compiler_params=pltpu.CompilerParams(vmem_limit_bytes=VMEM_BYTES),
        name="own_rows",
    )(place, *slices, panel, high, low, sq, panel_extra, own_extra)


def visit_kernel(cols, share, routes, place_ref, *refs):
    sources = sorted({name for route in routes for pick in route for name, _ in pick[1]})
    arrivals = dict(zip(sources, refs[: len(sources)]))
    slices = refs[len(sources) : len(sources) + cols]
    rest = refs[len(sources) + cols :]
    panel_hbm, high_hbm, low_hbm, block_high_hbm, block_low_hbm = rest[:5]
    sq_ref, half_ref, panel_extra_ref = rest[5:8]
    out_hbm = rest[9]
    seen, held, panel, high, low, block_high, block_low = rest[10:17]
    seen_high, seen_low, visit_half, tiles, sems = rest[17:]
    size = high.shape[0]
    row_count = size // share
    row, col = place_ref[0], place_ref[1]
    spot = lax.rem(row, LAYER)
    count = seen.shape[1]
    chunk = min(CHUNK, count)
    places = [lax.rem(col - d + cols, cols) for d in range(cols)]
    visits = len(routes)

    def arrive(v):
        for spots, parts, _ in routes[v]:
            chosen = spot == spots[0]
            for other in spots[1:]:
                chosen = chosen | (spot == other)

            @pl.when(chosen)
            def _():
                first = 0
                for name, length in parts:
                    pltpu.make_async_copy(
                        arrivals[name].at[0:length, :],
                        seen.at[v, first : first + length, :],
                        sems.at[v],
                    ).start()
                    first += length

    def arrived(v):
        pltpu.make_async_copy(seen.at[v], seen.at[v], sems.at[v]).wait()

    arrive(0)
    loads = [fetched(panel_hbm, panel, sems.at[visits])]
    loads.append(fetched(high_hbm, high, sems.at[visits + 1]))
    loads.append(fetched(low_hbm, low, sems.at[visits + 2]))
    for d in range(cols):
        piece = held.at[d * count : (d + 1) * count, :]
        loads.append(fetched(slices[d], piece, sems.at[visits + 3 + d]))
    loads.append(fetched(block_high_hbm, block_high, sems.at[visits + 3 + cols]))
    loads.append(fetched(block_low_hbm, block_low, sems.at[visits + 4 + cols]))
    for v in range(1, visits):
        arrive(v)
    sq_row = sq_ref[0:1, :]
    per = count // chunk

    def first_row(r):
        place = lax.rem(col - lax.div(r, per) + cols, cols)
        return pl.multiple_of(place * count + lax.rem(r, per) * chunk, chunk)

    def stop_of(v):
        stop = jnp.int32(0)
        for i, route in enumerate(routes):
            for spots, _, at_stop in route:
                for one in spots:
                    stop = jnp.where((spot == one) & (v == i), at_stop, stop)
        return stop

    def out_copy(v):
        first = pl.multiple_of(stop_of(v) * count, count)
        target = out_hbm.at[:, pl.ds(first, count)]
        return pltpu.make_async_copy(tiles.at[v], target, sems.at[visits + 5 + cols + v])

    loads[0].wait()

    def visit_step(v, carry):
        visit_row = lax.rem(row - stop_of(v) + row_count, row_count)
        arrived(v)
        visit_half[...] = jnp.broadcast_to(half_squares(seen[v]), (count, 128))

        def rows_step(r, carry):
            rows = pl.ds(pl.multiple_of(r * chunk, chunk), chunk)
            block = panel_rows(seen.at[v], rows, panel, places, visit_half[rows, 0:1], sq_row)
            block = panel_hits(block, col * count + r * chunk, visit_row, share, panel_extra_ref)

            @pl.when((v == 0) & (r == 0))
            def _():
                loads[1].wait()
                loads[2].wait()

            seen_high[rows, :], seen_low[rows, :] = split(solved(block, high, low))
            return carry

        lax.fori_loop(0, per, rows_step, 0)

        @pl.when(v == 0)
        def _():
            for load in loads[3:]:
                load.wait()

        visit_line = as_row(visit_half[:, 0:1])

        def tile_step(r, carry):
            rows = pl.ds(pl.multiple_of(r * chunk, chunk), chunk)
            there = pl.ds(first_row(r), chunk)
            inner = dot(held[rows, :], seen[v], NT)
            values = jnp.exp(inner - half_ref[there, 0:1] - visit_line)
            factor = (seen_high[...], seen_low[...])
            part = dot3((block_high[there, :], block_low[there, :]), factor, NT)
            tiles[v, there, :] = values - part
            return carry

        lax.fori_loop(0, cols * per, tile_step, 0)
        out_copy(v).start()
        return carry

    lax.fori_loop(0, visits, visit_step, 0)
    for v in range(visits):
        out_copy(v).wait()


def visit(name, routes, share, place, arrivals, slices, panel, own, panel_extra, trailing):
    sources = sorted({source for route in routes for pick in route for source, _ in pick[1]})
    cols = len(slices)
    (count, embed), visits = slices[0].shape, len(routes)
    block_rows = count * cols
    high, low, sq, block_high, block_low, half = own
    size = high.shape[0]
    vmem = pl.BlockSpec(memory_space=pltpu.VMEM)
    anywhere = pl.BlockSpec(memory_space=pl.ANY)
    moved = len(sources) + cols + 5
    return pl.pallas_call(
        functools.partial(visit_kernel, cols, share, routes),
        out_shape=jax.ShapeDtypeStruct(trailing.shape, F32),
        in_specs=[pl.BlockSpec(memory_space=pltpu.SMEM)]
        + [anywhere] * moved
        + [vmem] * 3
        + [anywhere],
        out_specs=anywhere,
        scratch_shapes=[
            pltpu.VMEM((visits, count, embed), BF16),
            pltpu.VMEM((block_rows, embed), BF16),
            pltpu.VMEM(panel.shape, BF16),
            pltpu.VMEM((size, size), BF16),
            pltpu.VMEM((size, size), BF16),
            pltpu.VMEM((block_rows, size), BF16),
            pltpu.VMEM((block_rows, size), BF16),
            pltpu.VMEM((count, size), BF16),
            pltpu.VMEM((count, size), BF16),
            pltpu.VMEM((count, 128), F32),
            pltpu.VMEM((visits, block_rows, count), F32),
            pltpu.SemaphoreType.DMA((2 * visits + 5 + cols,)),
        ],
        input_output_aliases={1 + moved + 3: 0},
        cost_estimate=pl.CostEstimate(
            flops=count * size, bytes_accessed=count * size, transcendentals=0
        ),
        compiler_params=pltpu.CompilerParams(vmem_limit_bytes=VMEM_BYTES),
        name=name,
    )(
        place,
        *[arrivals[source] for source in sources],
        *slices,
        panel,
        high,
        low,
        block_high,
        block_low,
        sq,
        half,
        panel_extra,
        trailing,
    )


def sent(block, pairs):
    return lax.ppermute(block, "row", pairs)


def after(value, *others):
    return lax.optimization_barrier((value,) + others)[0]


def body(embeddings, inverse_scales, matches):
    row_count = lax.axis_size("row")
    col_count = lax.axis_size("col")
    row_index = lax.axis_index("row")
    col_index = lax.axis_index("col")
    slice_rows, embed = embeddings.shape
    block_rows = slice_rows * col_count
    share = PANEL // row_count
    width = embed // col_count
    layers = row_count // LAYER
    rows = range(row_count)
    place = jnp.stack([row_index, col_index]).astype(jnp.int32)

    def spots(*wanted):
        return [r for r in rows if r % LAYER in wanted]

    def up(r):
        return (r + LAYER) % row_count

    part = jnp.where(col_index == 0, embeddings[:share, :width], jnp.zeros((share, width), BF16))
    for c in range(1, col_count):
        given = lax.ppermute(embeddings[:share, c * width : (c + 1) * width], "col", [(0, c)])
        part = jnp.where(col_index == c, given, part)
    own_scales = lax.dynamic_slice(inverse_scales, (col_index * width,), (width,))
    part = (part.astype(F32) * own_scales[None, :]).astype(BF16)
    scaled = (embeddings.astype(F32) * inverse_scales[None, :]).astype(BF16)
    column = [part]
    for back in range(1, layers):
        column.append(sent(part, [(r, (r + back * LAYER) % row_count) for r in rows]))
    column = jnp.concatenate(column, axis=0)
    extras = match_extras(after(matches, column), row_count * block_rows)
    gathered = [column] + [sent(column, [(r, r ^ d) for r in rows]) for d in range(1, LAYER)]
    gathered[1:] = [after(piece, extras, scaled) for piece in gathered[1:]]
    pieces = [gathered]
    for c in range(1, col_count):
        pieces.append([rotated(piece, "col", c) for piece in gathered])
    slices = [scaled] + [rotated(scaled, "col", d) for d in range(1, col_count)]

    extras = extras.reshape(row_count, block_rows)
    panel_extra = extras[:, :share].reshape(1, PANEL)
    own_extra = lax.dynamic_slice(
        extras, (row_index, col_index * slice_rows), (1, slice_rows)
    )

    rising = after(scaled, column)
    above = sent(rising, [(r, up(r)) for r in spots(1, 2, 3)])
    leaving = after(scaled, *gathered[1:])
    beside = sent(leaving, [(r, r ^ 1) for r in rows])
    across = sent(leaving, [(r, r ^ 2) for r in rows])

    high, low, sq, panel = inverse_lower(place, pieces, panel_extra, share)

    mid = slice_rows // 2
    spot = lax.rem(row_index, LAYER)
    beside2, across2, above2 = (after(block, high) for block in (beside, across, above))
    up2 = jnp.where(spot == 1, across2[:mid], beside2[mid:])
    x2 = jnp.where(spot == 2, across2[mid:], above2[:mid])
    y2 = jnp.where(spot == 2, above2[:mid], jnp.where(spot == 3, above2[mid:], beside2[:mid]))
    up2 = sent(up2, [(r, up(r)) for r in rows])
    x2 = sent(x2, [(r, r ^ 1) for r in spots(1, 2, 3)])
    y2 = sent(y2, [(r, r ^ 2) for r in rows])

    trailing, factor, block_high, block_low, half = own_rows(
        place, slices, panel, high, low, sq, panel_extra, own_extra, share
    )
    up2, x2, y2, half = lax.optimization_barrier((up2, x2, y2, half))
    x3 = jnp.where(spot == 1, up2, jnp.where(spot == 0, y2, across2[mid:]))
    up3 = sent(across2[mid:], [(r, up(r)) for r in spots(0)])
    x3 = sent(x3, [(r, r ^ 1) for r in spots(0, 1, 3)])
    y3 = sent(up2, [(r, r ^ 2) for r in spots(2, 3)])
    arrivals = {
        "across": across,
        "beside": beside,
        "up2": up2,
        "x2": x2,
        "y2": y2,
        "up3": up3,
        "x3": x3,
        "y3": y3,
    }

    def halves(low_half, high_half):
        return ((low_half, mid), (high_half, slice_rows - mid))

    def whole(block):
        return ((block, slice_rows),)

    first = (
        ((0,), halves("x2", "up2"), 3),
        ((1, 3), whole("beside"), 1),
        ((2,), whole("across"), 2),
    )
    second = (
        ((0,), halves("y2", "up3"), 2),
        ((1,), halves("up2", "y2"), 2),
        ((2,), halves("x2", "up2"), 3),
        ((3,), whole("across"), 2),
    )
    third = (
        ((0,), halves("x3", "y3"), 1),
        ((1,), halves("x3", "y3"), 3),
        ((2,), halves("y2", "x3"), 1),
        ((3,), halves("y2", "x2"), 3),
    )
    own = (high, low, sq, block_high, block_low, half)
    rest = (slices, panel, own, panel_extra)
    trailing = visit("visit_first", (first,), share, place, arrivals, *rest, trailing)
    trailing = visit("visit_rest", (second, third), share, place, arrivals, *rest, trailing)
    return (trailing, factor)


def solution(mesh):
    return jax.shard_map(
        body,
        mesh=mesh,
        in_specs=(P(("row", "col"), None), P(), P()),
        out_specs=(P("row", "col"), P(("row", "col"), None)),
        check_vma=False,
    )
```

```python
import functools

import jax
import jax.numpy as jnp
from jax import lax
from jax.experimental import pallas as pl
from jax.experimental.pallas import tpu as pltpu
from jax.sharding import PartitionSpec as P

PANEL = 1024
STOPS = 4
LAYER = 4
BLOCK = 128
GROUP = 8
CHUNK = 256
VMEM_BYTES = 56 * 1024 * 1024

F32 = jnp.float32
BF16 = jnp.bfloat16
NT = (((1,), (1,)), ((), ()))
NN = (((1,), (0,)), ((), ()))


def rotated(block, axis, distance):
    count = lax.axis_size(axis)
    return lax.ppermute(block, axis, [(i, (i + distance) % count) for i in range(count)])


def split(values):
    high = values.astype(BF16)
    low = (values - high.astype(F32)).astype(BF16)
    return high, low


def dot(left, right, dims):
    return lax.dot_general(left, right, dims, preferred_element_type=F32)


def dot3(left, right, dims):
    (lh, ll), (rh, rl) = left, right
    (left_dim,), (right_dim,) = dims[0]
    left = jnp.concatenate([lh, ll, lh], axis=left_dim)
    right = jnp.concatenate([rh, rh, rl], axis=right_dim)
    return dot(left, right, dims)


def half_squares(block):
    values = block.astype(F32)
    return 0.5 * jnp.sum(values * values, axis=1, keepdims=True)


def reciprocal(values):
    return pl.reciprocal(values, approx=True)


def fetched(source, target, sem):
    copy = pltpu.make_async_copy(source, target, sem)
    copy.start()
    return copy


def as_row(column):
    return jnp.transpose(jnp.broadcast_to(column, (column.shape[0], 128)))[0:1, :]


def iota(shape, dim):
    return lax.broadcasted_iota(jnp.int32, shape, dim)


def extras_kernel(chunk, matches_ref, out_ref):
    high_count = out_ref.shape[0]

    def step(i, total):
        for side in range(2):
            ids = matches_ref[side : side + 1, pl.ds(pl.multiple_of(i * chunk, chunk), chunk)]
            high = lax.shift_right_logical(ids, 7)
            low = jnp.bitwise_and(ids, 127)
            high_hot = jnp.where(iota((high_count, chunk), 0) == high, 1.0, 0.0).astype(BF16)
            low_hot = jnp.where(iota((128, chunk), 0) == low, 1.0, 0.0).astype(BF16)
            total = total + dot(high_hot, low_hot, NT)
        return total

    steps = matches_ref.shape[1] // chunk
    counts = lax.fori_loop(0, steps, step, jnp.zeros(out_ref.shape, F32))
    out_ref[...] = 0.1 + 0.5 * counts


def match_extras(matches, candidates):
    total = matches.shape[0]
    return pl.pallas_call(
        functools.partial(extras_kernel, min(total, 1024)),
        out_shape=jax.ShapeDtypeStruct((candidates // 128, 128), F32),
        in_specs=[pl.BlockSpec(memory_space=pltpu.VMEM)],
        out_specs=pl.BlockSpec(memory_space=pltpu.VMEM),
        cost_estimate=pl.CostEstimate(
            flops=8_000_000_000, bytes_accessed=total * 8, transcendentals=0
        ),
        compiler_params=pltpu.CompilerParams(vmem_limit_bytes=VMEM_BYTES),
        name="match_extras",
    )(matches.T)


def factor_block(diagonal, store):
    count = BLOCK // GROUP
    shape = (GROUP, BLOCK)
    sub = iota(shape, 0)
    lane = iota(shape, 1)
    rows = [diagonal[GROUP * i : GROUP * (i + 1), :] for i in range(count)]

    def column(values, index):
        return jnp.broadcast_to(values[:, index : index + 1], shape)

    def line(values, index):
        return jnp.broadcast_to(values[index : index + 1, :], shape)

    def pick(flags, values):
        result = values[0]
        for flag, value in zip(flags[1:], values[1:]):
            result = jnp.where(flag, value, result)
        return result

    at = [sub == j for j in range(GROUP)]
    for m in range(count):
        start = GROUP * m
        inside = (lane >= start) & (lane < start + GROUP)
        cols = [column(rows[m], start + b) for b in range(GROUP)]
        cell = {(a, b): line(cols[b], a) for b in range(GROUP) for a in range(b + 1)}
        held = jnp.where(inside, jnp.where(lane == start + sub, 1.0, 0.0), rows[m])
        lines = [line(held, j) for j in range(GROUP)]
        last = m + 1 == count
        if not last:
            near = [column(rows[m + 1], start + b) for b in range(GROUP)]
            change = None
        scaled_lines, factors, solved_lines, pivots = [], {}, [], []
        for j in range(0, GROUP, 2):
            top, cross, low = cell[j, j], cell[j, j + 1], cell[j + 1, j + 1]
            det = top * low - cross * cross
            inverse = reciprocal(det)
            tops, crosses, lows = top * inverse, cross * inverse, low * inverse
            for b in range(j + 2, GROUP):
                u, v = cell[j, b], cell[j + 1, b]
                factors[j, b] = u * lows - v * crosses
                factors[j + 1, b] = v * tops - u * crosses
            for b in range(j + 2, GROUP):
                for a in range(j + 2, b + 1):
                    part = factors[j, a] * cell[j, b] + factors[j + 1, a] * cell[j + 1, b]
                    cell[a, b] = cell[a, b] - part
            if not last:
                weight1 = near[j] * lows - near[j + 1] * crosses
                weight2 = near[j + 1] * tops - near[j] * crosses
                part = weight1 * lines[j] + weight2 * lines[j + 1]
                change = part if change is None else change + part
                for b in range(j + 2, GROUP):
                    near[b] = near[b] - (near[j] * factors[j, b] + near[j + 1] * factors[j + 1, b])
            for b in range(j + 2, GROUP):
                part = factors[j, b] * lines[j] + factors[j + 1, b] * lines[j + 1]
                lines[b] = lines[b] - part
            solved_lines.append(lines[j] * lows - lines[j + 1] * crosses)
            solved_lines.append(lines[j + 1] * tops - lines[j] * crosses)
            top_inverse = reciprocal(top)
            scaled_lines += [lines[j], lines[j + 1] - cross * top_inverse * lines[j]]
            pivots += [top, det * top_inverse]
        done = pick(at, scaled_lines) * lax.rsqrt(pick(at, pivots))
        store(m, jnp.where(lane < start + GROUP, done, 0.0))
        if not last:
            rows[m + 1] = jnp.where(inside, 0.0, rows[m + 1]) - change
            others = range(m + 2, count)
            for j in range(GROUP - 4, -1, -2) if len(others) > 0 else ():
                for b in range(j + 2, GROUP):
                    solved_lines[j] = solved_lines[j] - factors[j, b] * solved_lines[b]
                    solved_lines[j + 1] = solved_lines[j + 1] - factors[j + 1, b] * solved_lines[b]
            for i in others:
                terms = [column(rows[i], start + j) * solved_lines[j] for j in range(GROUP)]
                while len(terms) > 1:
                    terms = [a + b for a, b in zip(terms[0::2], terms[1::2])]
                rows[i] = jnp.where(inside, 0.0, rows[i]) - terms[0]


def lower_kernel(cols, layers, share, place_ref, *refs):
    pieces = refs[: cols * LAYER]
    extra_ref, high_ref, low_ref, sq_ref, panel_ref = refs[cols * LAYER : cols * LAYER + 5]
    panel, work, ahead, inv, inv_high, inv_low, sq_col, sems, panel_sem = refs[cols * LAYER + 5 :]
    size = work.shape[0]
    row, col = place_ref[0], place_ref[1]
    layer, spot = lax.div(row, LAYER), lax.rem(row, LAYER)
    width = panel.shape[1] // cols
    copies = []
    for e in range(cols):
        lanes = pl.ds(pl.multiple_of(lax.rem(col - e + cols, cols) * width, width), width)
        for d in range(LAYER):
            for back in range(layers):
                from_spot = spot + d - 2 * jnp.bitwise_and(spot, d)
                block = lax.rem(layer - back + layers, layers) * LAYER + from_spot
                there = pl.ds(pl.multiple_of(block * share, share), share)
                copies.append(
                    fetched(
                        pieces[e * LAYER + d].at[back * share : (back + 1) * share, :],
                        panel.at[there, lanes],
                        sems.at[len(copies)],
                    )
                )
    for copy in copies:
        copy.wait()
    saved = fetched(panel, panel_ref, panel_sem)
    tile = CHUNK
    for r in range(size // tile):
        rows = slice(r * tile, (r + 1) * tile)
        sq_col[rows, :] = jnp.broadcast_to(half_squares(panel[rows, :]), (tile, 128))
    sq_ref[...] = jnp.transpose(sq_col[...])[0:8, :]
    for r in range(size // tile):
        rows = slice(r * tile, (r + 1) * tile)
        inner = dot(panel[rows, :], panel[...], NT)
        block = jnp.exp(inner - sq_col[rows, 0:1] - sq_ref[0:1, :])
        on_diagonal = iota((tile, size), 0) + r * tile == iota((tile, size), 1)
        work[rows, :] = block + jnp.where(on_diagonal, extra_ref[...], 0.0)

    steps = size // BLOCK

    def place_of(k):
        return pl.ds(pl.multiple_of(k * BLOCK, BLOCK), BLOCK)

    def store(m, values):
        inv[GROUP * m : GROUP * (m + 1), :] = values

    def look_ahead(k):
        here, there = place_of(k), place_of(lax.rem(k + 1, steps))
        inverse = split(inv[...])
        inv_high[...], inv_low[...] = inverse
        factor = split(dot3(split(work[there, here]), inverse, NT))
        ahead[...] = work[there, there] - dot3(factor, factor, NT)

    def finish_line(k):
        here = place_of(k)
        inverse = (inv_high[...], inv_low[...])
        line = dot3(inverse, split(work[here, :]), NN)
        inside = lax.shift_right_logical(iota((BLOCK, size), 1), 7) == k
        whole = inv_high[...].astype(F32) + inv_low[...].astype(F32)
        line = jnp.where(inside, jnp.concatenate([whole] * steps, axis=1), line)
        work[here, :] = line
        return split(line)

    factor_block(work[0:BLOCK, 0:BLOCK], store)
    look_ahead(0)

    def eliminate(k, carry):
        here = place_of(k - 1)
        diagonal = ahead[...]
        inverse = (inv_high[...], inv_low[...])
        line = finish_line(k - 1)
        for d in range(steps - 1):
            there = place_of(lax.rem(k + d, steps))
            valid = k + d < steps
            factor = dot3(split(work[there, here]), inverse, NT)
            factor = split(jnp.where(valid, factor, 0.0))
            work[there, here] = jnp.where(valid, 0.0, work[there, here])
            work[there, :] = work[there, :] - dot3(factor, line, NN)
        factor_block(diagonal, store)
        look_ahead(k)
        return carry

    lax.fori_loop(1, steps, eliminate, 0)
    finish_line(steps - 1)
    for r in range(steps):
        rows = slice(r * BLOCK, (r + 1) * BLOCK)
        kept = iota((BLOCK, size), 0) + r * BLOCK >= iota((BLOCK, size), 1)
        high_ref[rows, :], low_ref[rows, :] = split(jnp.where(kept, work[rows, :], 0.0))
    saved.wait()


def inverse_lower(place, pieces, panel_extra, share):
    size = panel_extra.shape[1]
    cols = len(pieces)
    held, width = pieces[0][0].shape
    layers = held // share
    flat = [piece for group in pieces for piece in group]
    vmem = pl.BlockSpec(memory_space=pltpu.VMEM)
    anywhere = pl.BlockSpec(memory_space=pl.ANY)
    return pl.pallas_call(
        functools.partial(lower_kernel, cols, layers, share),
        out_shape=(
            jax.ShapeDtypeStruct((size, size), BF16),
            jax.ShapeDtypeStruct((size, size), BF16),
            jax.ShapeDtypeStruct((8, size), F32),
            jax.ShapeDtypeStruct((size, cols * width), BF16),
        ),
        in_specs=[pl.BlockSpec(memory_space=pltpu.SMEM)] + [anywhere] * len(flat) + [vmem],
        out_specs=(vmem, vmem, vmem, anywhere),
        scratch_shapes=[
            pltpu.VMEM((size, cols * width), BF16),
            pltpu.VMEM((size, size), F32),
            pltpu.VMEM((BLOCK, BLOCK), F32),
            pltpu.VMEM((BLOCK, BLOCK), F32),
            pltpu.VMEM((BLOCK, BLOCK), BF16),
            pltpu.VMEM((BLOCK, BLOCK), BF16),
            pltpu.VMEM((size, 128), F32),
            pltpu.SemaphoreType.DMA((cols * LAYER * layers,)),
            pltpu.SemaphoreType.DMA,
        ],
        cost_estimate=pl.CostEstimate(
            flops=50_000_000_000, bytes_accessed=8 * size * size, transcendentals=size * size
        ),
        compiler_params=pltpu.CompilerParams(vmem_limit_bytes=VMEM_BYTES),
        name="inverse_lower",
    )(place, *flat, panel_extra)


def solved(values, high_ref, low_ref):
    high, low = split(values)
    size = high.shape[1]
    parts = []
    for j in range(size // CHUNK):
        upto = CHUNK * (j + 1)
        rows = slice(CHUNK * j, upto)
        inverse = (high_ref[rows, :upto], low_ref[rows, :upto])
        parts.append(dot3((high[:, :upto], low[:, :upto]), inverse, NT))
    return jnp.concatenate(parts, axis=1)


def panel_rows(x, panel, half, sq_row, first_local, row, share, extra_ref):
    block = jnp.exp(dot(x, panel[...], NT) - half - sq_row)
    top = block[:share, :]
    local = iota(top.shape, 0) + first_local
    hit = (local + row * share == iota(top.shape, 1)) & (local < share)
    top = top + jnp.where(hit, extra_ref[...], 0.0)
    return jnp.concatenate([top, block[share:, :]], axis=0)


def own_kernel(cols, share, place_ref, *refs):
    slices = refs[:cols]
    panel_hbm, high_hbm, low_hbm, sq_ref, panel_extra_ref, own_extra_ref = refs[cols : cols + 6]
    out_hbm, factor_hbm, block_high_hbm, block_low_hbm, half_ref = refs[cols + 6 : cols + 11]
    held, panel, high, low, block_high, block_low, factor, tiles, sems = refs[cols + 11 :]
    row, col = place_ref[0], place_ref[1]
    count = held.shape[0] // cols
    chunk = min(CHUNK, count)

    copies = [fetched(slices[0], held.at[0:count, :], sems.at[0])]
    copies.append(fetched(panel_hbm, panel, sems.at[1]))
    copies += [fetched(high_hbm, high, sems.at[2]), fetched(low_hbm, low, sems.at[3])]
    for d in range(1, cols):
        copies.append(fetched(slices[d], held.at[d * count : (d + 1) * count, :], sems.at[3 + d]))
    per = count // chunk
    block_rows = cols * count
    for copy in copies:
        copy.wait()
    sq_row = sq_ref[0:1, :]

    def first_row(r):
        place = lax.rem(col - lax.div(r, per) + cols, cols)
        return pl.multiple_of(place * count + lax.rem(r, per) * chunk, chunk)

    def rows_step(d, carry):
        for i in range(per):
            r = d * per + i
            rows = pl.ds(pl.multiple_of(r * chunk, chunk), chunk)
            first = first_row(r)
            there = pl.ds(first, chunk)
            x = held[rows, :]
            half = half_squares(x)
            half_ref[there, :] = jnp.broadcast_to(half, (chunk, 128))
            block = panel_rows(x, panel, half, sq_row, first, row, share, panel_extra_ref)
            values = solved(block, high, low)
            factor[rows, :] = values
            block_high[there, :], block_low[there, :] = split(values)
        return carry

    lax.fori_loop(0, cols, rows_step, 0)
    outs = [
        fetched(factor.at[0:count, :], factor_hbm, sems.at[4 + cols]),
        fetched(block_high, block_high_hbm, sems.at[5 + cols]),
        fetched(block_low, block_low_hbm, sems.at[6 + cols]),
    ]
    mine = pl.ds(pl.multiple_of(col * count, count), count)
    own_row = as_row(half_ref[mine, 0:1])

    def tile_step(r, carry):
        rows = pl.ds(pl.multiple_of(r * chunk, chunk), chunk)
        there = pl.ds(first_row(r), chunk)
        inner = dot(held[rows, :], held[0:count, :], NT)
        values = jnp.exp(inner - half_ref[there, 0:1] - own_row)
        own_factor = (block_high[mine, :], block_low[mine, :])
        values = values - dot3((block_high[there, :], block_low[there, :]), own_factor, NT)
        same = iota((chunk, count), 0) + r * chunk == iota((chunk, count), 1)
        tiles[there, :] = values + jnp.where(same, own_extra_ref[...], 0.0)
        return carry

    lax.fori_loop(0, cols * per, tile_step, 0)
    outs.append(fetched(tiles, out_hbm.at[:, 0:count], sems.at[3 + cols]))
    for copy in outs:
        copy.wait()


def own_rows(place, slices, panel, high, low, sq, panel_extra, own_extra, share):
    cols = len(slices)
    (count, embed), size = slices[0].shape, high.shape[0]
    block_rows = count * cols
    vmem = pl.BlockSpec(memory_space=pltpu.VMEM)
    anywhere = pl.BlockSpec(memory_space=pl.ANY)
    return pl.pallas_call(
        functools.partial(own_kernel, cols, share),
        out_shape=(
            jax.ShapeDtypeStruct((block_rows, STOPS * count), F32),
            jax.ShapeDtypeStruct((count, size), F32),
            jax.ShapeDtypeStruct((block_rows, size), BF16),
            jax.ShapeDtypeStruct((block_rows, size), BF16),
            jax.ShapeDtypeStruct((block_rows, 128), F32),
        ),
        in_specs=[pl.BlockSpec(memory_space=pltpu.SMEM)] + [anywhere] * (cols + 3) + [vmem] * 3,
        out_specs=(anywhere, anywhere, anywhere, anywhere, vmem),
        scratch_shapes=[
            pltpu.VMEM((block_rows, embed), BF16),
            pltpu.VMEM(panel.shape, BF16),
            pltpu.VMEM((size, size), BF16),
            pltpu.VMEM((size, size), BF16),
            pltpu.VMEM((block_rows, size), BF16),
            pltpu.VMEM((block_rows, size), BF16),
            pltpu.VMEM((block_rows, size), F32),
            pltpu.VMEM((block_rows, count), F32),
            pltpu.SemaphoreType.DMA((cols + 7,)),
        ],
        cost_estimate=pl.CostEstimate(
            flops=block_rows * size, bytes_accessed=block_rows * size, transcendentals=0
        ),
        compiler_params=pltpu.CompilerParams(vmem_limit_bytes=VMEM_BYTES),
        name="own_rows",
    )(place, *slices, panel, high, low, sq, panel_extra, own_extra)


def visit_kernel(cols, share, routes, place_ref, *refs):
    sources = sorted({name for route in routes for pick in route for name, _ in pick[1]})
    arrivals = dict(zip(sources, refs[: len(sources)]))
    slices = refs[len(sources) : len(sources) + cols]
    rest = refs[len(sources) + cols :]
    panel_hbm, high_hbm, low_hbm, block_high_hbm, block_low_hbm = rest[:5]
    sq_ref, half_ref, panel_extra_ref = rest[5:8]
    out_hbm = rest[9]
    seen, held, panel, high, low, block_high, block_low = rest[10:17]
    seen_high, seen_low, visit_half, tiles, sems = rest[17:]
    size = high.shape[0]
    row_count = size // share
    row, col = place_ref[0], place_ref[1]
    spot = lax.rem(row, LAYER)
    count = seen.shape[1]
    chunk = min(CHUNK, count)
    visits = len(routes)

    def arrive(v):
        for spots, parts, _ in routes[v]:
            chosen = spot == spots[0]
            for other in spots[1:]:
                chosen = chosen | (spot == other)

            @pl.when(chosen)
            def _():
                first = 0
                for name, length in parts:
                    pltpu.make_async_copy(
                        arrivals[name].at[0:length, :],
                        seen.at[v, first : first + length, :],
                        sems.at[v],
                    ).start()
                    first += length

    def arrived(v):
        pltpu.make_async_copy(seen.at[v], seen.at[v], sems.at[v]).wait()

    arrive(0)
    loads = [fetched(panel_hbm, panel, sems.at[visits])]
    loads.append(fetched(high_hbm, high, sems.at[visits + 1]))
    loads.append(fetched(low_hbm, low, sems.at[visits + 2]))
    for d in range(cols):
        piece = held.at[d * count : (d + 1) * count, :]
        loads.append(fetched(slices[d], piece, sems.at[visits + 3 + d]))
    loads.append(fetched(block_high_hbm, block_high, sems.at[visits + 3 + cols]))
    loads.append(fetched(block_low_hbm, block_low, sems.at[visits + 4 + cols]))
    for v in range(1, visits):
        arrive(v)
    sq_row = sq_ref[0:1, :]
    per = count // chunk

    def first_row(r):
        place = lax.rem(col - lax.div(r, per) + cols, cols)
        return pl.multiple_of(place * count + lax.rem(r, per) * chunk, chunk)

    def stop_of(v):
        stop = jnp.int32(0)
        for i, route in enumerate(routes):
            for spots, _, at_stop in route:
                for one in spots:
                    stop = jnp.where((spot == one) & (v == i), at_stop, stop)
        return stop

    def out_copy(v):
        first = pl.multiple_of(stop_of(v) * count, count)
        target = out_hbm.at[:, pl.ds(first, count)]
        return pltpu.make_async_copy(tiles.at[v], target, sems.at[visits + 5 + cols + v])

    for load in loads[:3]:
        load.wait()

    def visit_step(v, carry):
        visit_row = lax.rem(row - stop_of(v) + row_count, row_count)
        arrived(v)
        visit_half[...] = jnp.broadcast_to(half_squares(seen[v]), (count, 128))

        for r in range(per):
            rows = slice(r * chunk, (r + 1) * chunk)
            first = col * count + r * chunk
            half = visit_half[rows, 0:1]
            x = seen[v, rows, :]
            block = panel_rows(x, panel, half, sq_row, first, visit_row, share, panel_extra_ref)
            seen_high[rows, :], seen_low[rows, :] = split(solved(block, high, low))

        @pl.when(v == 0)
        def _():
            for load in loads[3:]:
                load.wait()

        visit_line = as_row(visit_half[:, 0:1])

        def tile_step(r, carry):
            rows = pl.ds(pl.multiple_of(r * chunk, chunk), chunk)
            there = pl.ds(first_row(r), chunk)
            inner = dot(held[rows, :], seen[v], NT)
            values = jnp.exp(inner - half_ref[there, 0:1] - visit_line)
            factor = (seen_high[...], seen_low[...])
            part = dot3((block_high[there, :], block_low[there, :]), factor, NT)
            tiles[v, there, :] = values - part
            return carry

        lax.fori_loop(0, cols * per, tile_step, 0)
        out_copy(v).start()
        return carry

    lax.fori_loop(0, visits, visit_step, 0)
    for v in range(visits):
        out_copy(v).wait()


def visit(name, routes, share, place, arrivals, slices, panel, own, panel_extra, trailing):
    sources = sorted({source for route in routes for pick in route for source, _ in pick[1]})
    cols = len(slices)
    (count, embed), visits = slices[0].shape, len(routes)
    block_rows = count * cols
    high, low, sq, block_high, block_low, half = own
    size = high.shape[0]
    vmem = pl.BlockSpec(memory_space=pltpu.VMEM)
    anywhere = pl.BlockSpec(memory_space=pl.ANY)
    moved = len(sources) + cols + 5
    return pl.pallas_call(
        functools.partial(visit_kernel, cols, share, routes),
        out_shape=jax.ShapeDtypeStruct(trailing.shape, F32),
        in_specs=[pl.BlockSpec(memory_space=pltpu.SMEM)]
        + [anywhere] * moved
        + [vmem] * 3
        + [anywhere],
        out_specs=anywhere,
        scratch_shapes=[
            pltpu.VMEM((visits, count, embed), BF16),
            pltpu.VMEM((block_rows, embed), BF16),
            pltpu.VMEM(panel.shape, BF16),
            pltpu.VMEM((size, size), BF16),
            pltpu.VMEM((size, size), BF16),
            pltpu.VMEM((block_rows, size), BF16),
            pltpu.VMEM((block_rows, size), BF16),
            pltpu.VMEM((count, size), BF16),
            pltpu.VMEM((count, size), BF16),
            pltpu.VMEM((count, 128), F32),
            pltpu.VMEM((visits, block_rows, count), F32),
            pltpu.SemaphoreType.DMA((2 * visits + 5 + cols,)),
        ],
        input_output_aliases={1 + moved + 3: 0},
        cost_estimate=pl.CostEstimate(
            flops=count * size, bytes_accessed=count * size, transcendentals=0
        ),
        compiler_params=pltpu.CompilerParams(vmem_limit_bytes=VMEM_BYTES),
        name=name,
    )(
        place,
        *[arrivals[source] for source in sources],
        *slices,
        panel,
        high,
        low,
        block_high,
        block_low,
        sq,
        half,
        panel_extra,
        trailing,
    )


def sent(block, pairs):
    return lax.ppermute(block, "row", pairs)


def after(value, *others):
    return lax.optimization_barrier((value,) + others)[0]


def body(embeddings, inverse_scales, matches):
    row_count = lax.axis_size("row")
    col_count = lax.axis_size("col")
    row_index = lax.axis_index("row")
    col_index = lax.axis_index("col")
    slice_rows, embed = embeddings.shape
    block_rows = slice_rows * col_count
    share = PANEL // row_count
    width = embed // col_count
    layers = row_count // LAYER
    rows = range(row_count)
    place = jnp.stack([row_index, col_index]).astype(jnp.int32)

    def spots(*wanted):
        return [r for r in rows if r % LAYER in wanted]

    def up(r):
        return (r + LAYER) % row_count

    part = jnp.where(col_index == 0, embeddings[:share, :width], jnp.zeros((share, width), BF16))
    for c in range(1, col_count):
        given = lax.ppermute(embeddings[:share, c * width : (c + 1) * width], "col", [(0, c)])
        part = jnp.where(col_index == c, given, part)
    own_scales = lax.dynamic_slice(inverse_scales, (col_index * width,), (width,))
    part = (part.astype(F32) * own_scales[None, :]).astype(BF16)
    scaled = (embeddings.astype(F32) * inverse_scales[None, :]).astype(BF16)
    column = [part]
    for back in range(1, layers):
        column.append(sent(part, [(r, (r + back * LAYER) % row_count) for r in rows]))
    column = jnp.concatenate(column, axis=0)
    extras = match_extras(after(matches, column), row_count * block_rows)
    gathered = [column] + [sent(column, [(r, r ^ d) for r in rows]) for d in range(1, LAYER)]
    gathered[1:] = [after(piece, extras, scaled) for piece in gathered[1:]]
    pieces = [gathered]
    for c in range(1, col_count):
        pieces.append([rotated(piece, "col", c) for piece in gathered])
    slices = [scaled] + [rotated(scaled, "col", d) for d in range(1, col_count)]

    extras = extras.reshape(row_count, block_rows)
    panel_extra = extras[:, :share].reshape(1, PANEL)
    own_extra = lax.dynamic_slice(
        extras, (row_index, col_index * slice_rows), (1, slice_rows)
    )

    rising = after(scaled, column)
    above = sent(rising, [(r, up(r)) for r in spots(1, 2, 3)])
    leaving = after(scaled, *gathered[1:])
    beside = sent(leaving, [(r, r ^ 1) for r in rows])
    across = sent(leaving, [(r, r ^ 2) for r in rows])

    high, low, sq, panel = inverse_lower(place, pieces, panel_extra, share)

    mid = slice_rows // 2
    spot = lax.rem(row_index, LAYER)
    beside2, across2, above2 = (after(block, high) for block in (beside, across, above))
    up2 = jnp.where(spot == 1, across2[:mid], beside2[mid:])
    x2 = jnp.where(spot == 2, across2[mid:], above2[:mid])
    y2 = jnp.where(spot == 2, above2[:mid], jnp.where(spot == 3, above2[mid:], beside2[:mid]))
    up2 = sent(up2, [(r, up(r)) for r in rows])
    x2 = sent(x2, [(r, r ^ 1) for r in spots(1, 2, 3)])
    y2 = sent(y2, [(r, r ^ 2) for r in rows])

    trailing, factor, block_high, block_low, half = own_rows(
        place, slices, panel, high, low, sq, panel_extra, own_extra, share
    )
    up2, x2, y2, half = lax.optimization_barrier((up2, x2, y2, half))
    x3 = jnp.where(spot == 1, up2, jnp.where(spot == 0, y2, across2[mid:]))
    up3 = sent(across2[mid:], [(r, up(r)) for r in spots(0)])
    x3 = sent(x3, [(r, r ^ 1) for r in spots(0, 1, 3)])
    y3 = sent(up2, [(r, r ^ 2) for r in spots(2, 3)])
    arrivals = {
        "across": across,
        "beside": beside,
        "up2": up2,
        "x2": x2,
        "y2": y2,
        "up3": up3,
        "x3": x3,
        "y3": y3,
    }

    def halves(low_half, high_half):
        return ((low_half, mid), (high_half, slice_rows - mid))

    def whole(block):
        return ((block, slice_rows),)

    first = (
        ((0,), halves("x2", "up2"), 3),
        ((1, 3), whole("beside"), 1),
        ((2,), whole("across"), 2),
    )
    second = (
        ((0,), halves("y2", "up3"), 2),
        ((1,), halves("up2", "y2"), 2),
        ((2,), halves("x2", "up2"), 3),
        ((3,), whole("across"), 2),
    )
    third = (
        ((0,), halves("x3", "y3"), 1),
        ((1,), halves("x3", "y3"), 3),
        ((2,), halves("y2", "x3"), 1),
        ((3,), halves("y2", "x2"), 3),
    )
    own = (high, low, sq, block_high, block_low, half)
    rest = (slices, panel, own, panel_extra)
    trailing = visit("visit_first", (first,), share, place, arrivals, *rest, trailing)
    trailing = visit("visit_rest", (second, third), share, place, arrivals, *rest, trailing)
    return (trailing, factor)


def solution(mesh):
    return jax.shard_map(
        body,
        mesh=mesh,
        in_specs=(P(("row", "col"), None), P(), P()),
        out_specs=(P("row", "col"), P(("row", "col"), None)),
        check_vma=False,
    )
```

```python
import functools

import jax
import jax.numpy as jnp
from jax import lax
from jax.experimental import pallas as pl
from jax.experimental.pallas import tpu as pltpu
from jax.sharding import PartitionSpec as P

PANEL = 1024
STOPS = 4
LAYER = 4
BLOCK = 128
GROUP = 8
CUT = 6
CHUNK = 256
VMEM_BYTES = 56 * 1024 * 1024

F32 = jnp.float32
BF16 = jnp.bfloat16
NT = (((1,), (1,)), ((), ()))
NN = (((1,), (0,)), ((), ()))


def rotated(block, axis, distance):
    count = lax.axis_size(axis)
    return lax.ppermute(block, axis, [(i, (i + distance) % count) for i in range(count)])


def split(values):
    high = values.astype(BF16)
    low = (values - high.astype(F32)).astype(BF16)
    return high, low


def dot(left, right, dims):
    return lax.dot_general(left, right, dims, preferred_element_type=F32)


def dot3(left, right, dims):
    (lh, ll), (rh, rl) = left, right
    (left_dim,), (right_dim,) = dims[0]
    left = jnp.concatenate([lh, ll, lh], axis=left_dim)
    right = jnp.concatenate([rh, rh, rl], axis=right_dim)
    return dot(left, right, dims)


def half_squares(block):
    values = block.astype(F32)
    return 0.5 * jnp.sum(values * values, axis=1, keepdims=True)


def reciprocal(values):
    return pl.reciprocal(values, approx=True)


def fetched(source, target, sem):
    copy = pltpu.make_async_copy(source, target, sem)
    copy.start()
    return copy


def as_row(column):
    return jnp.transpose(jnp.broadcast_to(column, (column.shape[0], 128)))[0:1, :]


def iota(shape, dim):
    return lax.broadcasted_iota(jnp.int32, shape, dim)


def extras_kernel(chunk, matches_ref, out_ref):
    high_count = out_ref.shape[0]

    def step(i, total):
        for side in range(2):
            ids = matches_ref[side : side + 1, pl.ds(pl.multiple_of(i * chunk, chunk), chunk)]
            high = lax.shift_right_logical(ids, 7)
            low = jnp.bitwise_and(ids, 127)
            high_hot = jnp.where(iota((high_count, chunk), 0) == high, 1.0, 0.0).astype(BF16)
            low_hot = jnp.where(iota((128, chunk), 0) == low, 1.0, 0.0).astype(BF16)
            total = total + dot(high_hot, low_hot, NT)
        return total

    steps = matches_ref.shape[1] // chunk
    counts = lax.fori_loop(0, steps, step, jnp.zeros(out_ref.shape, F32))
    out_ref[...] = 0.1 + 0.5 * counts


def match_extras(matches, candidates):
    total = matches.shape[0]
    return pl.pallas_call(
        functools.partial(extras_kernel, min(total, 1024)),
        out_shape=jax.ShapeDtypeStruct((candidates // 128, 128), F32),
        in_specs=[pl.BlockSpec(memory_space=pltpu.VMEM)],
        out_specs=pl.BlockSpec(memory_space=pltpu.VMEM),
        cost_estimate=pl.CostEstimate(
            flops=8_000_000_000, bytes_accessed=total * 8, transcendentals=0
        ),
        compiler_params=pltpu.CompilerParams(vmem_limit_bytes=VMEM_BYTES),
        name="match_extras",
    )(matches.T)


def factor_block(diagonal, store):
    count = BLOCK // GROUP
    shape = (GROUP, BLOCK)
    sub = iota(shape, 0)
    lane = iota(shape, 1)
    rows = [diagonal[GROUP * i : GROUP * (i + 1), :] for i in range(count)]

    def column(values, index):
        return jnp.broadcast_to(values[:, index : index + 1], shape)

    def line(values, index):
        return jnp.broadcast_to(values[index : index + 1, :], shape)

    def pick(flags, values):
        result = values[0]
        for flag, value in zip(flags[1:], values[1:]):
            result = jnp.where(flag, value, result)
        return result

    at = [sub == j for j in range(GROUP)]
    for m in range(count):
        start = GROUP * m
        inside = (lane >= start) & (lane < start + GROUP)
        cols = [column(rows[m], start + b) for b in range(GROUP)]
        cell = {(a, b): line(cols[b], a) for b in range(GROUP) for a in range(b + 1)}
        held = jnp.where(inside, jnp.where(lane == start + sub, 1.0, 0.0), rows[m])
        lines = [line(held, j) for j in range(GROUP)]
        last = m + 1 == count
        if not last:
            near = [column(rows[m + 1], start + b) for b in range(GROUP)]
            change = None
        scaled_lines, factors, solved_lines, pivots = [], {}, [], []
        for j in range(0, GROUP, 2):
            top, cross, low = cell[j, j], cell[j, j + 1], cell[j + 1, j + 1]
            det = top * low - cross * cross
            inverse = reciprocal(det)
            tops, crosses, lows = top * inverse, cross * inverse, low * inverse
            for b in range(j + 2, GROUP):
                u, v = cell[j, b], cell[j + 1, b]
                factors[j, b] = u * lows - v * crosses
                factors[j + 1, b] = v * tops - u * crosses
            for b in range(j + 2, GROUP):
                for a in range(j + 2, b + 1):
                    part = factors[j, a] * cell[j, b] + factors[j + 1, a] * cell[j + 1, b]
                    cell[a, b] = cell[a, b] - part
            if not last:
                weight1 = near[j] * lows - near[j + 1] * crosses
                weight2 = near[j + 1] * tops - near[j] * crosses
                part = weight1 * lines[j] + weight2 * lines[j + 1]
                change = part if change is None else change + part
                for b in range(j + 2, GROUP):
                    near[b] = near[b] - (near[j] * factors[j, b] + near[j + 1] * factors[j + 1, b])
            for b in range(j + 2, GROUP):
                part = factors[j, b] * lines[j] + factors[j + 1, b] * lines[j + 1]
                lines[b] = lines[b] - part
            solved_lines.append(lines[j] * lows - lines[j + 1] * crosses)
            solved_lines.append(lines[j + 1] * tops - lines[j] * crosses)
            top_inverse = reciprocal(top)
            scaled_lines += [lines[j], lines[j + 1] - cross * top_inverse * lines[j]]
            pivots += [top, det * top_inverse]
        done = pick(at, scaled_lines) * lax.rsqrt(pick(at, pivots))
        store(m, jnp.where(lane < start + GROUP, done, 0.0))
        if not last:
            rows[m + 1] = jnp.where(inside, 0.0, rows[m + 1]) - change
            others = range(m + 2, count)
            for j in range(GROUP - 4, -1, -2) if len(others) > 0 else ():
                for b in range(j + 2, GROUP):
                    solved_lines[j] = solved_lines[j] - factors[j, b] * solved_lines[b]
                    solved_lines[j + 1] = solved_lines[j + 1] - factors[j + 1, b] * solved_lines[b]
            for i in others:
                terms = [column(rows[i], start + j) * solved_lines[j] for j in range(GROUP)]
                while len(terms) > 1:
                    terms = [a + b for a, b in zip(terms[0::2], terms[1::2])]
                rows[i] = jnp.where(inside, 0.0, rows[i]) - terms[0]


def elimination(work, ahead, inv, inv_high, inv_low):
    size = work.shape[0]
    steps = size // BLOCK

    def place_of(k):
        return pl.ds(pl.multiple_of(k * BLOCK, BLOCK), BLOCK)

    def store(m, values):
        inv[GROUP * m : GROUP * (m + 1), :] = values

    def look_ahead(k):
        here, there = place_of(k), place_of(lax.rem(k + 1, steps))
        inverse = split(inv[...])
        inv_high[...], inv_low[...] = inverse
        factor = split(dot3(split(work[there, here]), inverse, NT))
        ahead[...] = work[there, there] - dot3(factor, factor, NT)

    def finish_line(k):
        here = place_of(k)
        inverse = (inv_high[...], inv_low[...])
        line = dot3(inverse, split(work[here, :]), NN)
        inside = lax.shift_right_logical(iota((BLOCK, size), 1), 7) == k
        whole = inv_high[...].astype(F32) + inv_low[...].astype(F32)
        line = jnp.where(inside, jnp.concatenate([whole] * steps, axis=1), line)
        work[here, :] = line
        return split(line)

    def begin():
        factor_block(work[0:BLOCK, 0:BLOCK], store)
        look_ahead(0)

    def eliminate(k, carry):
        here = place_of(k - 1)
        diagonal = ahead[...]
        inverse = (inv_high[...], inv_low[...])
        line = finish_line(k - 1)
        for d in range(steps - 1):
            there = place_of(lax.rem(k + d, steps))
            valid = k + d < steps
            factor = dot3(split(work[there, here]), inverse, NT)
            factor = split(jnp.where(valid, factor, 0.0))
            work[there, here] = jnp.where(valid, 0.0, work[there, here])
            work[there, :] = work[there, :] - dot3(factor, line, NN)
        factor_block(diagonal, store)
        look_ahead(k)
        return carry

    return begin, eliminate, finish_line


def rest_kernel(work_hbm, ahead_in, inv_high_in, inv_low_in, high_ref, low_ref, *scratch):
    work, ahead, inv, inv_high, inv_low, sem = scratch
    fetched(work_hbm, work, sem).wait()
    ahead[...], inv_high[...], inv_low[...] = ahead_in[...], inv_high_in[...], inv_low_in[...]
    size = work.shape[0]
    steps = size // BLOCK
    _, eliminate, finish_line = elimination(work, ahead, inv, inv_high, inv_low)
    lax.fori_loop(CUT, steps, eliminate, 0)
    finish_line(steps - 1)
    for r in range(steps):
        rows = slice(r * BLOCK, (r + 1) * BLOCK)
        kept = iota((BLOCK, size), 0) + r * BLOCK >= iota((BLOCK, size), 1)
        high_ref[rows, :], low_ref[rows, :] = split(jnp.where(kept, work[rows, :], 0.0))


def finish_lower(state):
    work, ahead, inv_high, inv_low = state
    size = work.shape[0]
    vmem = pl.BlockSpec(memory_space=pltpu.VMEM)
    return pl.pallas_call(
        rest_kernel,
        out_shape=(jax.ShapeDtypeStruct((size, size), BF16),) * 2,
        in_specs=[pl.BlockSpec(memory_space=pl.ANY)] + [vmem] * 3,
        out_specs=(vmem, vmem),
        scratch_shapes=[
            pltpu.VMEM((size, size), F32),
            pltpu.VMEM((BLOCK, BLOCK), F32),
            pltpu.VMEM((BLOCK, BLOCK), F32),
            pltpu.VMEM((BLOCK, BLOCK), BF16),
            pltpu.VMEM((BLOCK, BLOCK), BF16),
            pltpu.SemaphoreType.DMA,
        ],
        cost_estimate=pl.CostEstimate(flops=size, bytes_accessed=size, transcendentals=0),
        compiler_params=pltpu.CompilerParams(vmem_limit_bytes=VMEM_BYTES),
        name="finish_lower",
    )(work, ahead, inv_high, inv_low)


def start_kernel(cols, layers, share, place_ref, *refs):
    pieces = refs[: cols * LAYER]
    extra_ref, sq_ref, panel_ref, work, ahead, inv_high, inv_low = refs[
        cols * LAYER : cols * LAYER + 7
    ]
    panel, inv, sq_col, sems, panel_sem = refs[cols * LAYER + 7 :]
    size = work.shape[0]
    row, col = place_ref[0], place_ref[1]
    layer, spot = lax.div(row, LAYER), lax.rem(row, LAYER)
    width = panel.shape[1] // cols
    copies = []
    for e in range(cols):
        lanes = pl.ds(pl.multiple_of(lax.rem(col - e + cols, cols) * width, width), width)
        for d in range(LAYER):
            for back in range(layers):
                from_spot = spot + d - 2 * jnp.bitwise_and(spot, d)
                block = lax.rem(layer - back + layers, layers) * LAYER + from_spot
                there = pl.ds(pl.multiple_of(block * share, share), share)
                copies.append(
                    fetched(
                        pieces[e * LAYER + d].at[back * share : (back + 1) * share, :],
                        panel.at[there, lanes],
                        sems.at[len(copies)],
                    )
                )
    for copy in copies:
        copy.wait()
    saved = fetched(panel, panel_ref, panel_sem)
    tile = CHUNK
    for r in range(size // tile):
        rows = slice(r * tile, (r + 1) * tile)
        sq_col[rows, :] = jnp.broadcast_to(half_squares(panel[rows, :]), (tile, 128))
    sq_ref[...] = jnp.transpose(sq_col[...])[0:8, :]
    for r in range(size // tile):
        rows = slice(r * tile, (r + 1) * tile)
        inner = dot(panel[rows, :], panel[...], NT)
        block = jnp.exp(inner - sq_col[rows, 0:1] - sq_ref[0:1, :])
        on_diagonal = iota((tile, size), 0) + r * tile == iota((tile, size), 1)
        work[rows, :] = block + jnp.where(on_diagonal, extra_ref[...], 0.0)

    begin, eliminate, _ = elimination(work, ahead, inv, inv_high, inv_low)
    begin()
    lax.fori_loop(1, CUT, eliminate, 0)
    saved.wait()


def start_lower(place, pieces, panel_extra, share):
    size = panel_extra.shape[1]
    cols = len(pieces)
    held, width = pieces[0][0].shape
    layers = held // share
    flat = [piece for group in pieces for piece in group]
    vmem = pl.BlockSpec(memory_space=pltpu.VMEM)
    anywhere = pl.BlockSpec(memory_space=pl.ANY)
    return pl.pallas_call(
        functools.partial(start_kernel, cols, layers, share),
        out_shape=(
            jax.ShapeDtypeStruct((8, size), F32),
            jax.ShapeDtypeStruct((size, cols * width), BF16),
            jax.ShapeDtypeStruct((size, size), F32),
            jax.ShapeDtypeStruct((BLOCK, BLOCK), F32),
            jax.ShapeDtypeStruct((BLOCK, BLOCK), BF16),
            jax.ShapeDtypeStruct((BLOCK, BLOCK), BF16),
        ),
        in_specs=[pl.BlockSpec(memory_space=pltpu.SMEM)] + [anywhere] * len(flat) + [vmem],
        out_specs=(vmem, anywhere, vmem, vmem, vmem, vmem),
        scratch_shapes=[
            pltpu.VMEM((size, cols * width), BF16),
            pltpu.VMEM((BLOCK, BLOCK), F32),
            pltpu.VMEM((size, 128), F32),
            pltpu.SemaphoreType.DMA((cols * LAYER * layers,)),
            pltpu.SemaphoreType.DMA,
        ],
        cost_estimate=pl.CostEstimate(
            flops=50_000_000_000, bytes_accessed=8 * size * size, transcendentals=size * size
        ),
        compiler_params=pltpu.CompilerParams(vmem_limit_bytes=VMEM_BYTES),
        name="start_lower",
    )(place, *flat, panel_extra)


def factor_rows(x, panel, half, sq_row, first_local, row, share, extra_ref, inverse):
    size = panel.shape[0]
    high_ref, low_ref = inverse

    def inner(j):
        return dot(x, panel[CHUNK * j : CHUNK * (j + 1), :], NT)

    def kernel_tile(j, products):
        lanes = slice(CHUNK * j, CHUNK * (j + 1))
        tile = jnp.exp(products - half - sq_row[:, lanes])
        top = tile[:share, :]
        local = iota(top.shape, 0) + first_local
        hit = (local + row * share == iota(top.shape, 1) + CHUNK * j) & (local < share)
        top = top + jnp.where(hit, extra_ref[:, lanes], 0.0)
        return split(jnp.concatenate([top, tile[share:, :]], axis=0))

    highs, lows, parts = [], [], []
    products = inner(0)
    for j in range(size // CHUNK):
        current = products
        if CHUNK * (j + 1) < size:
            products = inner(j + 1)
        high, low = kernel_tile(j, current)
        highs.append(high)
        lows.append(low)
        rows, upto = slice(CHUNK * j, CHUNK * (j + 1)), CHUNK * (j + 1)
        left = jnp.concatenate(highs + lows + highs, axis=1)
        inv_high, inv_low = high_ref[rows, :upto], low_ref[rows, :upto]
        right = jnp.concatenate([inv_high, inv_high, inv_low], axis=1)
        parts.append(dot(left, right, NT))
    return jnp.concatenate(parts, axis=1)


def own_kernel(cols, share, place_ref, *refs):
    slices = refs[:cols]
    panel_hbm, high_hbm, low_hbm, sq_ref, panel_extra_ref, own_extra_ref = refs[cols : cols + 6]
    out_hbm, factor_hbm, block_high_hbm, block_low_hbm, half_ref = refs[cols + 6 : cols + 11]
    held, panel, high, low, block_high, block_low, factor, tiles, sems = refs[cols + 11 :]
    row, col = place_ref[0], place_ref[1]
    count = held.shape[0] // cols
    chunk = min(CHUNK, count)

    copies = [fetched(slices[0], held.at[0:count, :], sems.at[0])]
    copies.append(fetched(panel_hbm, panel, sems.at[1]))
    copies += [fetched(high_hbm, high, sems.at[2]), fetched(low_hbm, low, sems.at[3])]
    for d in range(1, cols):
        copies.append(fetched(slices[d], held.at[d * count : (d + 1) * count, :], sems.at[3 + d]))
    per = count // chunk
    block_rows = cols * count
    for copy in copies:
        copy.wait()
    sq_row = sq_ref[0:1, :]

    def first_row(r):
        place = lax.rem(col - lax.div(r, per) + cols, cols)
        return pl.multiple_of(place * count + lax.rem(r, per) * chunk, chunk)

    def rows_step(d, carry):
        for i in range(per):
            r = d * per + i
            rows = pl.ds(pl.multiple_of(r * chunk, chunk), chunk)
            first = first_row(r)
            there = pl.ds(first, chunk)
            x = held[rows, :]
            half = half_squares(x)
            half_ref[there, :] = jnp.broadcast_to(half, (chunk, 128))
            values = factor_rows(
                x, panel, half, sq_row, first, row, share, panel_extra_ref, (high, low)
            )
            factor[rows, :] = values
            block_high[there, :], block_low[there, :] = split(values)
        return carry

    lax.fori_loop(0, cols, rows_step, 0)
    outs = [
        fetched(factor.at[0:count, :], factor_hbm, sems.at[4 + cols]),
        fetched(block_high, block_high_hbm, sems.at[5 + cols]),
        fetched(block_low, block_low_hbm, sems.at[6 + cols]),
    ]
    mine = pl.ds(pl.multiple_of(col * count, count), count)
    own_row = as_row(half_ref[mine, 0:1])

    def tile_step(r, carry):
        rows = pl.ds(pl.multiple_of(r * chunk, chunk), chunk)
        there = pl.ds(first_row(r), chunk)
        inner = dot(held[rows, :], held[0:count, :], NT)
        values = jnp.exp(inner - half_ref[there, 0:1] - own_row)
        own_factor = (block_high[mine, :], block_low[mine, :])
        values = values - dot3((block_high[there, :], block_low[there, :]), own_factor, NT)
        same = iota((chunk, count), 0) + r * chunk == iota((chunk, count), 1)
        tiles[there, :] = values + jnp.where(same, own_extra_ref[...], 0.0)
        return carry

    lax.fori_loop(0, cols * per, tile_step, 0)
    outs.append(fetched(tiles, out_hbm.at[:, 0:count], sems.at[3 + cols]))
    for copy in outs:
        copy.wait()


def own_rows(place, slices, panel, high, low, sq, panel_extra, own_extra, share):
    cols = len(slices)
    (count, embed), size = slices[0].shape, high.shape[0]
    block_rows = count * cols
    vmem = pl.BlockSpec(memory_space=pltpu.VMEM)
    anywhere = pl.BlockSpec(memory_space=pl.ANY)
    return pl.pallas_call(
        functools.partial(own_kernel, cols, share),
        out_shape=(
            jax.ShapeDtypeStruct((block_rows, STOPS * count), F32),
            jax.ShapeDtypeStruct((count, size), F32),
            jax.ShapeDtypeStruct((block_rows, size), BF16),
            jax.ShapeDtypeStruct((block_rows, size), BF16),
            jax.ShapeDtypeStruct((block_rows, 128), F32),
        ),
        in_specs=[pl.BlockSpec(memory_space=pltpu.SMEM)] + [anywhere] * (cols + 3) + [vmem] * 3,
        out_specs=(anywhere, anywhere, anywhere, anywhere, vmem),
        scratch_shapes=[
            pltpu.VMEM((block_rows, embed), BF16),
            pltpu.VMEM(panel.shape, BF16),
            pltpu.VMEM((size, size), BF16),
            pltpu.VMEM((size, size), BF16),
            pltpu.VMEM((block_rows, size), BF16),
            pltpu.VMEM((block_rows, size), BF16),
            pltpu.VMEM((block_rows, size), F32),
            pltpu.VMEM((block_rows, count), F32),
            pltpu.SemaphoreType.DMA((cols + 7,)),
        ],
        cost_estimate=pl.CostEstimate(
            flops=block_rows * size, bytes_accessed=block_rows * size, transcendentals=0
        ),
        compiler_params=pltpu.CompilerParams(vmem_limit_bytes=VMEM_BYTES),
        name="own_rows",
    )(place, *slices, panel, high, low, sq, panel_extra, own_extra)


def visit_kernel(cols, share, routes, place_ref, *refs):
    sources = sorted({name for route in routes for pick in route for name, _ in pick[1]})
    arrivals = dict(zip(sources, refs[: len(sources)]))
    slices = refs[len(sources) : len(sources) + cols]
    rest = refs[len(sources) + cols :]
    panel_hbm, high_hbm, low_hbm, block_high_hbm, block_low_hbm = rest[:5]
    sq_ref, half_ref, panel_extra_ref = rest[5:8]
    out_hbm = rest[9]
    seen, held, panel, high, low, block_high, block_low = rest[10:17]
    seen_high, seen_low, visit_half, tiles, sems = rest[17:]
    size = high.shape[0]
    row_count = size // share
    row, col = place_ref[0], place_ref[1]
    spot = lax.rem(row, LAYER)
    count = seen.shape[1]
    chunk = min(CHUNK, count)
    visits = len(routes)

    def arrive(v):
        for spots, parts, _ in routes[v]:
            chosen = spot == spots[0]
            for other in spots[1:]:
                chosen = chosen | (spot == other)

            @pl.when(chosen)
            def _():
                first = 0
                for name, length in parts:
                    pltpu.make_async_copy(
                        arrivals[name].at[0:length, :],
                        seen.at[v, first : first + length, :],
                        sems.at[v],
                    ).start()
                    first += length

    def arrived(v):
        pltpu.make_async_copy(seen.at[v], seen.at[v], sems.at[v]).wait()

    arrive(0)
    loads = [fetched(panel_hbm, panel, sems.at[visits])]
    loads.append(fetched(high_hbm, high, sems.at[visits + 1]))
    loads.append(fetched(low_hbm, low, sems.at[visits + 2]))
    for d in range(cols):
        piece = held.at[d * count : (d + 1) * count, :]
        loads.append(fetched(slices[d], piece, sems.at[visits + 3 + d]))
    loads.append(fetched(block_high_hbm, block_high, sems.at[visits + 3 + cols]))
    loads.append(fetched(block_low_hbm, block_low, sems.at[visits + 4 + cols]))
    for v in range(1, visits):
        arrive(v)
    sq_row = sq_ref[0:1, :]
    per = count // chunk

    def first_row(r):
        place = lax.rem(col - lax.div(r, per) + cols, cols)
        return pl.multiple_of(place * count + lax.rem(r, per) * chunk, chunk)

    def stop_of(v):
        stop = jnp.int32(0)
        for i, route in enumerate(routes):
            for spots, _, at_stop in route:
                for one in spots:
                    stop = jnp.where((spot == one) & (v == i), at_stop, stop)
        return stop

    def out_copy(v):
        first = pl.multiple_of(stop_of(v) * count, count)
        target = out_hbm.at[:, pl.ds(first, count)]
        return pltpu.make_async_copy(tiles.at[v], target, sems.at[visits + 5 + cols + v])

    for load in loads[:3]:
        load.wait()

    def visit_step(v, carry):
        visit_row = lax.rem(row - stop_of(v) + row_count, row_count)
        arrived(v)
        visit_half[...] = jnp.broadcast_to(half_squares(seen[v]), (count, 128))

        for r in range(per):
            rows = slice(r * chunk, (r + 1) * chunk)
            first = col * count + r * chunk
            half = visit_half[rows, 0:1]
            x = seen[v, rows, :]
            values = factor_rows(
                x, panel, half, sq_row, first, visit_row, share, panel_extra_ref, (high, low)
            )
            seen_high[rows, :], seen_low[rows, :] = split(values)

        @pl.when(v == 0)
        def _():
            for load in loads[3:]:
                load.wait()

        visit_line = as_row(visit_half[:, 0:1])

        def tile_step(r, carry):
            rows = pl.ds(pl.multiple_of(r * chunk, chunk), chunk)
            there = pl.ds(first_row(r), chunk)
            inner = dot(held[rows, :], seen[v], NT)
            values = jnp.exp(inner - half_ref[there, 0:1] - visit_line)
            factor = (seen_high[...], seen_low[...])
            part = dot3((block_high[there, :], block_low[there, :]), factor, NT)
            tiles[v, there, :] = values - part
            return carry

        lax.fori_loop(0, cols * per, tile_step, 0)
        out_copy(v).start()
        return carry

    lax.fori_loop(0, visits, visit_step, 0)
    for v in range(visits):
        out_copy(v).wait()


def visit(name, routes, share, place, arrivals, slices, panel, own, panel_extra, trailing):
    sources = sorted({source for route in routes for pick in route for source, _ in pick[1]})
    cols = len(slices)
    (count, embed), visits = slices[0].shape, len(routes)
    block_rows = count * cols
    high, low, sq, block_high, block_low, half = own
    size = high.shape[0]
    vmem = pl.BlockSpec(memory_space=pltpu.VMEM)
    anywhere = pl.BlockSpec(memory_space=pl.ANY)
    moved = len(sources) + cols + 5
    return pl.pallas_call(
        functools.partial(visit_kernel, cols, share, routes),
        out_shape=jax.ShapeDtypeStruct(trailing.shape, F32),
        in_specs=[pl.BlockSpec(memory_space=pltpu.SMEM)]
        + [anywhere] * moved
        + [vmem] * 3
        + [anywhere],
        out_specs=anywhere,
        scratch_shapes=[
            pltpu.VMEM((visits, count, embed), BF16),
            pltpu.VMEM((block_rows, embed), BF16),
            pltpu.VMEM(panel.shape, BF16),
            pltpu.VMEM((size, size), BF16),
            pltpu.VMEM((size, size), BF16),
            pltpu.VMEM((block_rows, size), BF16),
            pltpu.VMEM((block_rows, size), BF16),
            pltpu.VMEM((count, size), BF16),
            pltpu.VMEM((count, size), BF16),
            pltpu.VMEM((count, 128), F32),
            pltpu.VMEM((visits, block_rows, count), F32),
            pltpu.SemaphoreType.DMA((2 * visits + 5 + cols,)),
        ],
        input_output_aliases={1 + moved + 3: 0},
        cost_estimate=pl.CostEstimate(
            flops=count * size, bytes_accessed=count * size, transcendentals=0
        ),
        compiler_params=pltpu.CompilerParams(vmem_limit_bytes=VMEM_BYTES),
        name=name,
    )(
        place,
        *[arrivals[source] for source in sources],
        *slices,
        panel,
        high,
        low,
        block_high,
        block_low,
        sq,
        half,
        panel_extra,
        trailing,
    )


def sent(block, pairs):
    return lax.ppermute(block, "row", pairs)


def after(value, *others):
    return lax.optimization_barrier((value,) + others)[0]


def body(embeddings, inverse_scales, matches):
    row_count = lax.axis_size("row")
    col_count = lax.axis_size("col")
    row_index = lax.axis_index("row")
    col_index = lax.axis_index("col")
    slice_rows, embed = embeddings.shape
    block_rows = slice_rows * col_count
    share = PANEL // row_count
    width = embed // col_count
    layers = row_count // LAYER
    rows = range(row_count)
    place = jnp.stack([row_index, col_index]).astype(jnp.int32)

    def spots(*wanted):
        return [r for r in rows if r % LAYER in wanted]

    def up(r):
        return (r + LAYER) % row_count

    part = jnp.where(col_index == 0, embeddings[:share, :width], jnp.zeros((share, width), BF16))
    for c in range(1, col_count):
        given = lax.ppermute(embeddings[:share, c * width : (c + 1) * width], "col", [(0, c)])
        part = jnp.where(col_index == c, given, part)
    own_scales = lax.dynamic_slice(inverse_scales, (col_index * width,), (width,))
    part = (part.astype(F32) * own_scales[None, :]).astype(BF16)
    scaled = (embeddings.astype(F32) * inverse_scales[None, :]).astype(BF16)
    column = [part]
    for back in range(1, layers):
        column.append(sent(part, [(r, (r + back * LAYER) % row_count) for r in rows]))
    column = jnp.concatenate(column, axis=0)
    extras = match_extras(after(matches, column), row_count * block_rows)
    gathered = [column] + [sent(column, [(r, r ^ d) for r in rows]) for d in range(1, LAYER)]
    gathered[1:] = [after(piece, extras, scaled) for piece in gathered[1:]]
    pieces = [gathered]
    for c in range(1, col_count):
        pieces.append([rotated(piece, "col", c) for piece in gathered])
    slices = [scaled] + [rotated(scaled, "col", d) for d in range(1, col_count)]

    extras = extras.reshape(row_count, block_rows)
    panel_extra = extras[:, :share].reshape(1, PANEL)
    own_extra = lax.dynamic_slice(
        extras, (row_index, col_index * slice_rows), (1, slice_rows)
    )

    rising = after(scaled, column)
    above = sent(rising, [(r, up(r)) for r in spots(1, 2, 3)])
    leaving = after(scaled, *gathered[1:])
    beside = sent(leaving, [(r, r ^ 1) for r in rows])
    across = sent(leaving, [(r, r ^ 2) for r in rows])

    sq, panel, *state = start_lower(place, pieces, panel_extra, share)

    mid = slice_rows // 2
    spot = lax.rem(row_index, LAYER)
    beside2, across2, above2 = (after(block, *state) for block in (beside, across, above))
    up2 = jnp.where(spot == 1, across2[:mid], beside2[mid:])
    x2 = jnp.where(spot == 2, across2[mid:], above2[:mid])
    y2 = jnp.where(spot == 2, above2[:mid], jnp.where(spot == 3, above2[mid:], beside2[:mid]))
    up2 = sent(up2, [(r, up(r)) for r in rows])
    x2 = sent(x2, [(r, r ^ 1) for r in spots(1, 2, 3)])
    y2 = sent(y2, [(r, r ^ 2) for r in rows])

    high, low = finish_lower(state)
    up2, x2, y2, high = lax.optimization_barrier((up2, x2, y2, high))
    x3 = jnp.where(spot == 1, up2, jnp.where(spot == 0, y2, across2[mid:]))
    up3 = sent(across2[mid:], [(r, up(r)) for r in spots(0)])
    x3 = sent(x3, [(r, r ^ 1) for r in spots(0, 1, 3)])
    y3 = sent(up2, [(r, r ^ 2) for r in spots(2, 3)])
    trailing, factor, block_high, block_low, half = own_rows(
        place, slices, panel, high, low, sq, panel_extra, own_extra, share
    )
    arrivals = {
        "across": across,
        "beside": beside,
        "up2": up2,
        "x2": x2,
        "y2": y2,
        "up3": up3,
        "x3": x3,
        "y3": y3,
    }

    def halves(low_half, high_half):
        return ((low_half, mid), (high_half, slice_rows - mid))

    def whole(block):
        return ((block, slice_rows),)

    first = (
        ((0,), halves("x2", "up2"), 3),
        ((1, 3), whole("beside"), 1),
        ((2,), whole("across"), 2),
    )
    second = (
        ((0,), halves("y2", "up3"), 2),
        ((1,), halves("up2", "y2"), 2),
        ((2,), halves("x2", "up2"), 3),
        ((3,), whole("across"), 2),
    )
    third = (
        ((0,), halves("x3", "y3"), 1),
        ((1,), halves("x3", "y3"), 3),
        ((2,), halves("y2", "x3"), 1),
        ((3,), halves("y2", "x2"), 3),
    )
    own = (high, low, sq, block_high, block_low, half)
    rest = (slices, panel, own, panel_extra)
    routes = (first, second, third)
    trailing = visit("visit_all", routes, share, place, arrivals, *rest, trailing)
    return (trailing, factor)


def solution(mesh):
    return jax.shard_map(
        body,
        mesh=mesh,
        in_specs=(P(("row", "col"), None), P(), P()),
        out_specs=(P("row", "col"), P(("row", "col"), None)),
        check_vma=False,
    )
```

```python
import functools

import jax
import jax.numpy as jnp
from jax import lax
from jax.experimental import pallas as pl
from jax.experimental.pallas import tpu as pltpu
from jax.sharding import PartitionSpec as P

PANEL = 1024
STOPS = 4
LAYER = 4
BLOCK = 128
GROUP = 8
CHUNK = 256
VMEM_BYTES = 56 * 1024 * 1024

F32 = jnp.float32
BF16 = jnp.bfloat16
NT = (((1,), (1,)), ((), ()))
NN = (((1,), (0,)), ((), ()))


def rotated(block, axis, distance):
    count = lax.axis_size(axis)
    return lax.ppermute(block, axis, [(i, (i + distance) % count) for i in range(count)])


def split(values):
    high = values.astype(BF16)
    low = (values - high.astype(F32)).astype(BF16)
    return high, low


def dot(left, right, dims):
    return lax.dot_general(left, right, dims, preferred_element_type=F32)


def dot3(left, right, dims):
    (lh, ll), (rh, rl) = left, right
    (left_dim,), (right_dim,) = dims[0]
    left = jnp.concatenate([lh, ll, lh], axis=left_dim)
    right = jnp.concatenate([rh, rh, rl], axis=right_dim)
    return dot(left, right, dims)


def half_squares(block):
    values = block.astype(F32)
    return 0.5 * jnp.sum(values * values, axis=1, keepdims=True)


def reciprocal(values):
    return pl.reciprocal(values, approx=True)


def fetched(source, target, sem):
    copy = pltpu.make_async_copy(source, target, sem)
    copy.start()
    return copy


def as_row(column):
    return jnp.transpose(jnp.broadcast_to(column, (column.shape[0], 128)))[0:1, :]


def iota(shape, dim):
    return lax.broadcasted_iota(jnp.int32, shape, dim)


def extras_kernel(chunk, matches_ref, out_ref):
    high_count = out_ref.shape[0]

    def step(i, total):
        for side in range(2):
            ids = matches_ref[side : side + 1, pl.ds(pl.multiple_of(i * chunk, chunk), chunk)]
            high = lax.shift_right_logical(ids, 7)
            low = jnp.bitwise_and(ids, 127)
            high_hot = jnp.where(iota((high_count, chunk), 0) == high, 1.0, 0.0).astype(BF16)
            low_hot = jnp.where(iota((128, chunk), 0) == low, 1.0, 0.0).astype(BF16)
            total = total + dot(high_hot, low_hot, NT)
        return total

    steps = matches_ref.shape[1] // chunk
    counts = lax.fori_loop(0, steps, step, jnp.zeros(out_ref.shape, F32))
    out_ref[...] = 0.1 + 0.5 * counts


def match_extras(matches, candidates):
    total = matches.shape[0]
    return pl.pallas_call(
        functools.partial(extras_kernel, min(total, 1024)),
        out_shape=jax.ShapeDtypeStruct((candidates // 128, 128), F32),
        in_specs=[pl.BlockSpec(memory_space=pltpu.VMEM)],
        out_specs=pl.BlockSpec(memory_space=pltpu.VMEM),
        cost_estimate=pl.CostEstimate(
            flops=8_000_000_000, bytes_accessed=total * 8, transcendentals=0
        ),
        compiler_params=pltpu.CompilerParams(vmem_limit_bytes=VMEM_BYTES),
        name="match_extras",
    )(matches.T)


def factor_block(diagonal, store):
    count = BLOCK // GROUP
    shape = (GROUP, BLOCK)
    sub = iota(shape, 0)
    lane = iota(shape, 1)
    rows = [diagonal[GROUP * i : GROUP * (i + 1), :] for i in range(count)]

    def column(values, index):
        return jnp.broadcast_to(values[:, index : index + 1], shape)

    def line(values, index):
        return jnp.broadcast_to(values[index : index + 1, :], shape)

    def pick(flags, values):
        result = values[0]
        for flag, value in zip(flags[1:], values[1:]):
            result = jnp.where(flag, value, result)
        return result

    at = [sub == j for j in range(GROUP)]
    for m in range(count):
        start = GROUP * m
        inside = (lane >= start) & (lane < start + GROUP)
        cols = [column(rows[m], start + b) for b in range(GROUP)]
        cell = {(a, b): line(cols[b], a) for b in range(GROUP) for a in range(b + 1)}
        held = jnp.where(inside, jnp.where(lane == start + sub, 1.0, 0.0), rows[m])
        lines = [line(held, j) for j in range(GROUP)]
        last = m + 1 == count
        if not last:
            near = [column(rows[m + 1], start + b) for b in range(GROUP)]
            change = None
        scaled_lines, factors, solved_lines, pivots = [], {}, [], []
        for j in range(0, GROUP, 2):
            top, cross, low = cell[j, j], cell[j, j + 1], cell[j + 1, j + 1]
            det = top * low - cross * cross
            inverse = reciprocal(det)
            tops, crosses, lows = top * inverse, cross * inverse, low * inverse
            for b in range(j + 2, GROUP):
                u, v = cell[j, b], cell[j + 1, b]
                factors[j, b] = u * lows - v * crosses
                factors[j + 1, b] = v * tops - u * crosses
            for b in range(j + 2, GROUP):
                for a in range(j + 2, b + 1):
                    part = factors[j, a] * cell[j, b] + factors[j + 1, a] * cell[j + 1, b]
                    cell[a, b] = cell[a, b] - part
            if not last:
                weight1 = near[j] * lows - near[j + 1] * crosses
                weight2 = near[j + 1] * tops - near[j] * crosses
                part = weight1 * lines[j] + weight2 * lines[j + 1]
                change = part if change is None else change + part
                for b in range(j + 2, GROUP):
                    near[b] = near[b] - (near[j] * factors[j, b] + near[j + 1] * factors[j + 1, b])
            for b in range(j + 2, GROUP):
                part = factors[j, b] * lines[j] + factors[j + 1, b] * lines[j + 1]
                lines[b] = lines[b] - part
            solved_lines.append(lines[j] * lows - lines[j + 1] * crosses)
            solved_lines.append(lines[j + 1] * tops - lines[j] * crosses)
            top_inverse = reciprocal(top)
            scaled_lines += [lines[j], lines[j + 1] - cross * top_inverse * lines[j]]
            pivots += [top, det * top_inverse]
        done = pick(at, scaled_lines) * lax.rsqrt(pick(at, pivots))
        store(m, jnp.where(lane < start + GROUP, done, 0.0))
        if not last:
            rows[m + 1] = jnp.where(inside, 0.0, rows[m + 1]) - change
            others = range(m + 2, count)
            for j in range(GROUP - 4, -1, -2) if len(others) > 0 else ():
                for b in range(j + 2, GROUP):
                    solved_lines[j] = solved_lines[j] - factors[j, b] * solved_lines[b]
                    solved_lines[j + 1] = solved_lines[j + 1] - factors[j + 1, b] * solved_lines[b]
            for i in others:
                terms = [column(rows[i], start + j) * solved_lines[j] for j in range(GROUP)]
                while len(terms) > 1:
                    terms = [a + b for a, b in zip(terms[0::2], terms[1::2])]
                rows[i] = jnp.where(inside, 0.0, rows[i]) - terms[0]


def lower_kernel(cols, layers, share, place_ref, *refs):
    pieces = refs[: cols * LAYER]
    extra_ref, high_ref, low_ref, sq_ref, panel_ref = refs[cols * LAYER : cols * LAYER + 5]
    panel, work, ahead, inv, inv_high, inv_low, sq_col, sems, panel_sem = refs[cols * LAYER + 5 :]
    size = work.shape[0]
    row, col = place_ref[0], place_ref[1]
    layer, spot = lax.div(row, LAYER), lax.rem(row, LAYER)
    width = panel.shape[1] // cols
    copies = []
    for e in range(cols):
        lanes = pl.ds(pl.multiple_of(lax.rem(col - e + cols, cols) * width, width), width)
        for d in range(LAYER):
            for back in range(layers):
                from_spot = spot + d - 2 * jnp.bitwise_and(spot, d)
                block = lax.rem(layer - back + layers, layers) * LAYER + from_spot
                there = pl.ds(pl.multiple_of(block * share, share), share)
                copies.append(
                    fetched(
                        pieces[e * LAYER + d].at[back * share : (back + 1) * share, :],
                        panel.at[there, lanes],
                        sems.at[len(copies)],
                    )
                )
    for copy in copies:
        copy.wait()
    saved = fetched(panel, panel_ref, panel_sem)
    tile = CHUNK
    for r in range(size // tile):
        rows = slice(r * tile, (r + 1) * tile)
        sq_col[rows, :] = jnp.broadcast_to(half_squares(panel[rows, :]), (tile, 128))
    sq_ref[...] = jnp.transpose(sq_col[...])[0:8, :]
    for r in range(size // tile):
        rows = slice(r * tile, (r + 1) * tile)
        inner = dot(panel[rows, :], panel[...], NT)
        block = jnp.exp(inner - sq_col[rows, 0:1] - sq_ref[0:1, :])
        on_diagonal = iota((tile, size), 0) + r * tile == iota((tile, size), 1)
        work[rows, :] = block + jnp.where(on_diagonal, extra_ref[...], 0.0)

    steps = size // BLOCK

    def place_of(k):
        return pl.ds(pl.multiple_of(k * BLOCK, BLOCK), BLOCK)

    def store(m, values):
        inv[GROUP * m : GROUP * (m + 1), :] = values

    def look_ahead(k):
        here, there = place_of(k), place_of(lax.rem(k + 1, steps))
        inverse = split(inv[...])
        inv_high[...], inv_low[...] = inverse
        factor = split(dot3(split(work[there, here]), inverse, NT))
        ahead[...] = work[there, there] - dot3(factor, factor, NT)

    def finish_line(k):
        here = place_of(k)
        inverse = (inv_high[...], inv_low[...])
        line = dot3(inverse, split(work[here, :]), NN)
        inside = lax.shift_right_logical(iota((BLOCK, size), 1), 7) == k
        whole = inv_high[...].astype(F32) + inv_low[...].astype(F32)
        line = jnp.where(inside, jnp.concatenate([whole] * steps, axis=1), line)
        work[here, :] = line
        return split(line)

    factor_block(work[0:BLOCK, 0:BLOCK], store)
    look_ahead(0)

    def eliminate(k, carry):
        here = place_of(k - 1)
        diagonal = ahead[...]
        inverse = (inv_high[...], inv_low[...])
        line = finish_line(k - 1)
        for d in range(steps - 1):
            there = place_of(lax.rem(k + d, steps))
            valid = k + d < steps
            factor = dot3(split(work[there, here]), inverse, NT)
            factor = split(jnp.where(valid, factor, 0.0))
            work[there, here] = jnp.where(valid, 0.0, work[there, here])
            work[there, :] = work[there, :] - dot3(factor, line, NN)
        factor_block(diagonal, store)
        look_ahead(k)
        return carry

    lax.fori_loop(1, steps, eliminate, 0)
    finish_line(steps - 1)
    for r in range(steps):
        rows = slice(r * BLOCK, (r + 1) * BLOCK)
        kept = iota((BLOCK, size), 0) + r * BLOCK >= iota((BLOCK, size), 1)
        high_ref[rows, :], low_ref[rows, :] = split(jnp.where(kept, work[rows, :], 0.0))
    saved.wait()


def inverse_lower(place, pieces, panel_extra, share):
    size = panel_extra.shape[1]
    cols = len(pieces)
    held, width = pieces[0][0].shape
    layers = held // share
    flat = [piece for group in pieces for piece in group]
    vmem = pl.BlockSpec(memory_space=pltpu.VMEM)
    anywhere = pl.BlockSpec(memory_space=pl.ANY)
    return pl.pallas_call(
        functools.partial(lower_kernel, cols, layers, share),
        out_shape=(
            jax.ShapeDtypeStruct((size, size), BF16),
            jax.ShapeDtypeStruct((size, size), BF16),
            jax.ShapeDtypeStruct((8, size), F32),
            jax.ShapeDtypeStruct((size, cols * width), BF16),
        ),
        in_specs=[pl.BlockSpec(memory_space=pltpu.SMEM)] + [anywhere] * len(flat) + [vmem],
        out_specs=(vmem, vmem, vmem, anywhere),
        scratch_shapes=[
            pltpu.VMEM((size, cols * width), BF16),
            pltpu.VMEM((size, size), F32),
            pltpu.VMEM((BLOCK, BLOCK), F32),
            pltpu.VMEM((BLOCK, BLOCK), F32),
            pltpu.VMEM((BLOCK, BLOCK), BF16),
            pltpu.VMEM((BLOCK, BLOCK), BF16),
            pltpu.VMEM((size, 128), F32),
            pltpu.SemaphoreType.DMA((cols * LAYER * layers,)),
            pltpu.SemaphoreType.DMA,
        ],
        cost_estimate=pl.CostEstimate(
            flops=50_000_000_000, bytes_accessed=8 * size * size, transcendentals=size * size
        ),
        compiler_params=pltpu.CompilerParams(vmem_limit_bytes=VMEM_BYTES),
        name="inverse_lower",
    )(place, *flat, panel_extra)


class Loads:
    def __init__(self, sems):
        self.sems, self.used, self.waiting = sems, 0, {}

    def start(self, name, source, target):
        copy = fetched(source, target, self.sems.at[self.used])
        self.used += 1
        self.waiting.setdefault(name, []).append(copy)

    def ready(self, *name):
        for copy in self.waiting.pop(name, []):
            copy.wait()

    def constants(self, panel_hbm, high_hbm, low_hbm, panel, high, low):
        for j in range(panel.shape[0] // CHUNK):
            rows, upto = slice(CHUNK * j, CHUNK * (j + 1)), CHUNK * (j + 1)
            self.start(("panel", j), panel_hbm.at[rows, :], panel.at[rows, :])
            self.start(("inverse", j), high_hbm.at[rows, :upto], high.at[rows, :upto])
            self.start(("inverse", j), low_hbm.at[rows, :upto], low.at[rows, :upto])


def nothing(*name):
    pass


def row_of_chunk(r, col, cols, count, chunk):
    per = count // chunk
    place = lax.rem(col - lax.div(r, per) + cols, cols)
    return pl.multiple_of(place * count + lax.rem(r, per) * chunk, chunk)


def factor_rows(x, panel, half, sq_row, first_local, row, share, extra_ref, inverse, ready):
    size = panel.shape[0]
    high_ref, low_ref = inverse

    def inner(j):
        ready("panel", j)
        return dot(x, panel[CHUNK * j : CHUNK * (j + 1), :], NT)

    def kernel_tile(j, products):
        lanes = slice(CHUNK * j, CHUNK * (j + 1))
        tile = jnp.exp(products - half - sq_row[:, lanes])
        top = tile[:share, :]
        local = iota(top.shape, 0) + first_local
        hit = (local + row * share == iota(top.shape, 1) + CHUNK * j) & (local < share)
        top = top + jnp.where(hit, extra_ref[:, lanes], 0.0)
        return split(jnp.concatenate([top, tile[share:, :]], axis=0))

    highs, lows, parts = [], [], []
    products = inner(0)
    for j in range(size // CHUNK):
        current = products
        if CHUNK * (j + 1) < size:
            products = inner(j + 1)
        high, low = kernel_tile(j, current)
        highs.append(high)
        lows.append(low)
        ready("inverse", j)
        rows, upto = slice(CHUNK * j, CHUNK * (j + 1)), CHUNK * (j + 1)
        left = jnp.concatenate(highs + lows + highs, axis=1)
        inv_high, inv_low = high_ref[rows, :upto], low_ref[rows, :upto]
        right = jnp.concatenate([inv_high, inv_high, inv_low], axis=1)
        parts.append(dot(left, right, NT))
    return jnp.concatenate(parts, axis=1)


def own_kernel(cols, share, place_ref, *refs):
    slices = refs[:cols]
    panel_hbm, high_hbm, low_hbm, sq_ref, panel_extra_ref = refs[cols : cols + 5]
    factor_hbm, block_high_hbm, block_low_hbm, half_hbm = refs[cols + 5 : cols + 9]
    held, panel, high, low, block_high, block_low, half_ref, factor, sems = refs[cols + 9 :]
    row, col = place_ref[0], place_ref[1]
    count = held.shape[0] // cols
    chunk = min(CHUNK, count)
    per = count // chunk
    loads = Loads(sems)
    loads.start(("slice", 0), slices[0], held.at[0:count, :])
    loads.constants(panel_hbm, high_hbm, low_hbm, panel, high, low)
    for d in range(1, cols):
        loads.start(("slice", d), slices[d], held.at[d * count : (d + 1) * count, :])
    sq_row = sq_ref[0:1, :]

    def rows_step(r, ready):
        rows = pl.ds(pl.multiple_of(r * chunk, chunk), chunk)
        first = row_of_chunk(r, col, cols, count, chunk)
        there = pl.ds(first, chunk)
        x = held[rows, :]
        half = half_squares(x)
        half_ref[there, :] = jnp.broadcast_to(half, (chunk, 128))
        values = factor_rows(
            x, panel, half, sq_row, first, row, share, panel_extra_ref, (high, low), ready
        )
        factor[rows, :] = values
        block_high[there, :], block_low[there, :] = split(values)

    def later_step(r, carry):
        rows_step(r, nothing)
        return carry

    loads.ready("slice", 0)
    rows_step(jnp.int32(0), loads.ready)
    for d in range(1, cols):
        loads.ready("slice", d)
    lax.fori_loop(1, cols * per, later_step, 0)
    loads.start(("out",), factor.at[0:count, :], factor_hbm)
    loads.start(("out",), block_high, block_high_hbm)
    loads.start(("out",), block_low, block_low_hbm)
    loads.start(("out",), half_ref, half_hbm)
    loads.ready("out")


def own_factor(place, slices, panel, high, low, sq, panel_extra, share):
    cols = len(slices)
    (count, embed), size = slices[0].shape, high.shape[0]
    block_rows = count * cols
    vmem = pl.BlockSpec(memory_space=pltpu.VMEM)
    anywhere = pl.BlockSpec(memory_space=pl.ANY)
    return pl.pallas_call(
        functools.partial(own_kernel, cols, share),
        out_shape=(
            jax.ShapeDtypeStruct((count, size), F32),
            jax.ShapeDtypeStruct((block_rows, size), BF16),
            jax.ShapeDtypeStruct((block_rows, size), BF16),
            jax.ShapeDtypeStruct((block_rows, 128), F32),
        ),
        in_specs=[pl.BlockSpec(memory_space=pltpu.SMEM)] + [anywhere] * (cols + 3) + [vmem] * 2,
        out_specs=(anywhere,) * 4,
        scratch_shapes=[
            pltpu.VMEM((block_rows, embed), BF16),
            pltpu.VMEM(panel.shape, BF16),
            pltpu.VMEM((size, size), BF16),
            pltpu.VMEM((size, size), BF16),
            pltpu.VMEM((block_rows, size), BF16),
            pltpu.VMEM((block_rows, size), BF16),
            pltpu.VMEM((block_rows, 128), F32),
            pltpu.VMEM((block_rows, size), F32),
            pltpu.SemaphoreType.DMA((cols + 3 * (size // CHUNK) + 4,)),
        ],
        cost_estimate=pl.CostEstimate(
            flops=block_rows * size, bytes_accessed=block_rows * size, transcendentals=0
        ),
        compiler_params=pltpu.CompilerParams(vmem_limit_bytes=VMEM_BYTES),
        name="own_factor",
    )(place, *slices, panel, high, low, sq, panel_extra)


def visit_kernel(cols, share, routes, with_own, place_ref, *refs):
    sources = sorted({name for route in routes for pick in route for name, _ in pick[1]})
    arrivals = dict(zip(sources, refs[: len(sources)]))
    slices = refs[len(sources) : len(sources) + cols]
    rest = refs[len(sources) + cols :]
    panel_hbm, high_hbm, low_hbm, block_high_hbm, block_low_hbm, half_hbm = rest[:6]
    sq_ref, panel_extra_ref, own_extra_ref = rest[6:9]
    rest = rest[9:] if with_own else rest[10:]
    out_hbm, seen, held, panel, high, low, block_high, block_low, half_ref = rest[:9]
    seen_high, seen_low, tiles, sems = rest[9:]
    size = high.shape[0]
    row_count = size // share
    row, col = place_ref[0], place_ref[1]
    spot = lax.rem(row, LAYER)
    count = seen.shape[1]
    chunk = min(CHUNK, count)
    per = count // chunk
    visits = len(routes)

    def arrive(v):
        for spots, parts, _ in routes[v]:
            chosen = spot == spots[0]
            for other in spots[1:]:
                chosen = chosen | (spot == other)

            @pl.when(chosen)
            def _():
                first = 0
                for name, length in parts:
                    pltpu.make_async_copy(
                        arrivals[name].at[0:length, :],
                        seen.at[v, first : first + length, :],
                        sems.at[v],
                    ).start()
                    first += length

    arrive(0)
    loads = Loads(sems)
    loads.used = visits
    loads.constants(panel_hbm, high_hbm, low_hbm, panel, high, low)
    for d in range(cols):
        loads.start(("block",), slices[d], held.at[d * count : (d + 1) * count, :])
    loads.start(("block",), half_hbm, half_ref)
    loads.start(("block",), block_high_hbm, block_high)
    loads.start(("block",), block_low_hbm, block_low)
    for v in range(1, visits):
        arrive(v)
    sq_row = sq_ref[0:1, :]

    def tile_rows(slot, x, x_row, factor, own):
        for r in range(cols * per):
            rows = slice(r * chunk, (r + 1) * chunk)
            there = pl.ds(row_of_chunk(r, col, cols, count, chunk), chunk)
            inner = dot(held[rows, :], x, NT)
            values = jnp.exp(inner - half_ref[there, 0:1] - x_row)
            values = values - dot3((block_high[there, :], block_low[there, :]), factor, NT)
            if own and r < per:
                same = iota((chunk, count), 0) + r * chunk == iota((chunk, count), 1)
                values = values + jnp.where(same, own_extra_ref[...], 0.0)
            tiles[slot, there, :] = values

    for v in range(visits):
        stop = jnp.int32(0)
        for spots, _, at_stop in routes[v]:
            for one in spots:
                stop = jnp.where(spot == one, at_stop, stop)
        visit_row = lax.rem(row - stop + row_count, row_count)
        pltpu.make_async_copy(seen.at[v], seen.at[v], sems.at[v]).wait()
        half = half_squares(seen[v])
        for r in range(per):
            rows = slice(r * chunk, (r + 1) * chunk)
            first = col * count + r * chunk
            values = factor_rows(
                seen[v, rows, :],
                panel,
                half[rows, :],
                sq_row,
                first,
                visit_row,
                share,
                panel_extra_ref,
                (high, low),
                loads.ready,
            )
            seen_high[rows, :], seen_low[rows, :] = split(values)
        loads.ready("block")
        tile_rows(v, seen[v], as_row(half), (seen_high[...], seen_low[...]), False)
        target = out_hbm.at[:, pl.ds(pl.multiple_of(stop * count, count), count)]
        loads.start(("out",), tiles.at[v], target)
    if with_own:
        mine = pl.ds(pl.multiple_of(col * count, count), count)
        factor = (block_high[mine, :], block_low[mine, :])
        tile_rows(visits, held[0:count, :], as_row(half_ref[mine, 0:1]), factor, True)
        loads.start(("out",), tiles.at[visits], out_hbm.at[:, 0:count])
    loads.ready("out")


def visit(name, routes, share, place, arrivals, slices, panel, own, extras, trailing):
    sources = sorted({source for route in routes for pick in route for source, _ in pick[1]})
    cols = len(slices)
    (count, embed), visits = slices[0].shape, len(routes)
    block_rows = count * cols
    high, low, sq, block_high, block_low, half = own
    size = high.shape[0]
    with_own = trailing is None
    slots = visits + (1 if with_own else 0)
    vmem = pl.BlockSpec(memory_space=pltpu.VMEM)
    anywhere = pl.BlockSpec(memory_space=pl.ANY)
    moved = len(sources) + cols + 6
    operands = [
        place,
        *[arrivals[source] for source in sources],
        *slices,
        panel,
        high,
        low,
        block_high,
        block_low,
        half,
        sq,
        *extras,
    ]
    in_specs = [pl.BlockSpec(memory_space=pltpu.SMEM)] + [anywhere] * moved + [vmem] * 3
    aliases = {}
    if not with_own:
        operands.append(trailing)
        in_specs.append(anywhere)
        aliases = {1 + moved + 3: 0}
    return pl.pallas_call(
        functools.partial(visit_kernel, cols, share, routes, with_own),
        out_shape=jax.ShapeDtypeStruct((block_rows, STOPS * count), F32),
        in_specs=in_specs,
        out_specs=anywhere,
        scratch_shapes=[
            pltpu.VMEM((visits, count, embed), BF16),
            pltpu.VMEM((block_rows, embed), BF16),
            pltpu.VMEM(panel.shape, BF16),
            pltpu.VMEM((size, size), BF16),
            pltpu.VMEM((size, size), BF16),
            pltpu.VMEM((block_rows, size), BF16),
            pltpu.VMEM((block_rows, size), BF16),
            pltpu.VMEM((block_rows, 128), F32),
            pltpu.VMEM((count, size), BF16),
            pltpu.VMEM((count, size), BF16),
            pltpu.VMEM((slots, block_rows, count), F32),
            pltpu.SemaphoreType.DMA((visits + 3 * (size // CHUNK) + cols + 3 + slots,)),
        ],
        input_output_aliases=aliases,
        cost_estimate=pl.CostEstimate(
            flops=count * size, bytes_accessed=count * size, transcendentals=0
        ),
        compiler_params=pltpu.CompilerParams(vmem_limit_bytes=VMEM_BYTES),
        name=name,
    )(*operands)


def sent(block, pairs):
    return lax.ppermute(block, "row", pairs)


def after(value, *others):
    return lax.optimization_barrier((value,) + others)[0]


def body(embeddings, inverse_scales, matches):
    row_count = lax.axis_size("row")
    col_count = lax.axis_size("col")
    row_index = lax.axis_index("row")
    col_index = lax.axis_index("col")
    slice_rows, embed = embeddings.shape
    block_rows = slice_rows * col_count
    share = PANEL // row_count
    width = embed // col_count
    layers = row_count // LAYER
    rows = range(row_count)
    place = jnp.stack([row_index, col_index]).astype(jnp.int32)

    def spots(*wanted):
        return [r for r in rows if r % LAYER in wanted]

    def up(r):
        return (r + LAYER) % row_count

    part = jnp.where(col_index == 0, embeddings[:share, :width], jnp.zeros((share, width), BF16))
    for c in range(1, col_count):
        given = lax.ppermute(embeddings[:share, c * width : (c + 1) * width], "col", [(0, c)])
        part = jnp.where(col_index == c, given, part)
    own_scales = lax.dynamic_slice(inverse_scales, (col_index * width,), (width,))
    part = (part.astype(F32) * own_scales[None, :]).astype(BF16)
    scaled = (embeddings.astype(F32) * inverse_scales[None, :]).astype(BF16)
    column = [part]
    for back in range(1, layers):
        column.append(sent(part, [(r, (r + back * LAYER) % row_count) for r in rows]))
    column = jnp.concatenate(column, axis=0)
    extras = match_extras(after(matches, column), row_count * block_rows)
    gathered = [column] + [sent(column, [(r, r ^ d) for r in rows]) for d in range(1, LAYER)]
    gathered[1:] = [after(piece, extras, scaled) for piece in gathered[1:]]
    pieces = [gathered]
    for c in range(1, col_count):
        pieces.append([rotated(piece, "col", c) for piece in gathered])
    slices = [scaled] + [rotated(scaled, "col", d) for d in range(1, col_count)]

    extras = extras.reshape(row_count, block_rows)
    panel_extra = extras[:, :share].reshape(1, PANEL)
    own_extra = lax.dynamic_slice(
        extras, (row_index, col_index * slice_rows), (1, slice_rows)
    )

    rising = after(scaled, column)
    above = sent(rising, [(r, up(r)) for r in spots(1, 2, 3)])
    leaving = after(scaled, *gathered[1:])
    beside = sent(leaving, [(r, r ^ 1) for r in rows])
    across = sent(leaving, [(r, r ^ 2) for r in rows])

    high, low, sq, panel = inverse_lower(place, pieces, panel_extra, share)

    mid = slice_rows // 2
    spot = lax.rem(row_index, LAYER)
    beside2, across2, above2 = (after(block, high) for block in (beside, across, above))
    up2 = jnp.where(spot == 1, across2[:mid], beside2[mid:])
    x2 = jnp.where(spot == 2, across2[mid:], above2[:mid])
    y2 = jnp.where(spot == 2, above2[:mid], jnp.where(spot == 3, above2[mid:], beside2[:mid]))
    up2 = sent(up2, [(r, up(r)) for r in rows])
    x2 = sent(x2, [(r, r ^ 1) for r in spots(1, 2, 3)])
    y2 = sent(y2, [(r, r ^ 2) for r in rows])

    factor, block_high, block_low, half = own_factor(
        place, slices, panel, high, low, sq, panel_extra, share
    )
    up2, x2, y2, half = lax.optimization_barrier((up2, x2, y2, half))
    x3 = jnp.where(spot == 1, up2, jnp.where(spot == 0, y2, across2[mid:]))
    up3 = sent(across2[mid:], [(r, up(r)) for r in spots(0)])
    x3 = sent(x3, [(r, r ^ 1) for r in spots(0, 1, 3)])
    y3 = sent(up2, [(r, r ^ 2) for r in spots(2, 3)])
    arrivals = {
        "across": across,
        "beside": beside,
        "up2": up2,
        "x2": x2,
        "y2": y2,
        "up3": up3,
        "x3": x3,
        "y3": y3,
    }

    def halves(low_half, high_half):
        return ((low_half, mid), (high_half, slice_rows - mid))

    def whole(block):
        return ((block, slice_rows),)

    first = (
        ((0,), halves("x2", "up2"), 3),
        ((1, 3), whole("beside"), 1),
        ((2,), whole("across"), 2),
    )
    second = (
        ((0,), halves("y2", "up3"), 2),
        ((1,), halves("up2", "y2"), 2),
        ((2,), halves("x2", "up2"), 3),
        ((3,), whole("across"), 2),
    )
    third = (
        ((0,), halves("x3", "y3"), 1),
        ((1,), halves("x3", "y3"), 3),
        ((2,), halves("y2", "x3"), 1),
        ((3,), halves("y2", "x2"), 3),
    )
    own = (high, low, sq, block_high, block_low, half)
    rest = (slices, panel, own, (panel_extra, own_extra))
    trailing = visit("own_and_first", (first,), share, place, arrivals, *rest, None)
    trailing = visit("visit_rest", (second, third), share, place, arrivals, *rest, trailing)
    return (trailing, factor)


def solution(mesh):
    return jax.shard_map(
        body,
        mesh=mesh,
        in_specs=(P(("row", "col"), None), P(), P()),
        out_specs=(P("row", "col"), P(("row", "col"), None)),
        check_vma=False,
    )
```
